256 devices in a mesh: rep: 64 (over x, z, core), fsdp: 4 (over y).
Axes of the slice: x: 4, y: 4, z: 8, core: 2. Of those that a mesh axis runs over, the one named last changes fastest.
Arguments:
- grads: bfloat16 [64, 128, 27648], P('rep', None, 'fsdp')
- momentum: float32 [64, 128, 27648], P('rep', None, 'fsdp'), may hold values from -6 to 6
- master: float32 [128, 27648], P(None, 'fsdp'), may hold values from -6 to 6
- band_index: int32 [64, 2, 6912], P(None, None, 'fsdp'), may hold values from 0 to 4095, as said below
Outputs:
- new_momentum: float32 [64, 128, 27648], P('rep', None, 'fsdp')
- update: float32 [128, 27648], P(None, 'fsdp')
- weights_full: bfloat16 [128, 27648], replicated
The draws below stay inside these ranges and needn't reach their ends.
Inputs may be any that keep to these rules, and one draw needn't show every extreme that they name: `band_index`: the j-th index of each block lies in [j * 64 * 4, (j + 1) * 64 * 4), so a block's indices are distinct.
All inputs are finite; a program needn't handle non-finite values.
Results may differ from the reference program's by a relative error of at most 0.001.
Values may be sent and summed in bfloat16 or wider, within the bound.
A program may use at most 128 MiB of HBM per device.

```python
import math
import jax
import jax.numpy as jnp
from jax import lax

COLS = 27648
ROWS = 128
BLOCK = 64
BAND = 16
REPLICAS = 64


def draw_grads(key, part):
    key = jax.random.fold_in(key, 11)
    first, second, third = jax.random.split(key, 3)
    shape = (REPLICAS, ROWS, COLS)
    base = jax.random.normal(first, shape, jnp.float32)
    low, high = (math.log(0.3), math.log(3.0))
    row_scale = jnp.exp(jax.random.uniform(second, (REPLICAS, ROWS, 1), jnp.float32, low, high))
    col_scale = jnp.exp(jax.random.uniform(third, (1, 1, COLS), jnp.float32, low, high))
    return (base * row_scale * col_scale).astype(jnp.bfloat16)


def draw_band_index(key, part):
    key = jax.random.fold_in(key, 23)
    stride = BLOCK * BLOCK // BAND
    shape = (REPLICAS, ROWS // BLOCK, COLS // BLOCK * BAND)
    offset = jax.random.randint(key, shape, 0, stride, dtype=jnp.int32)
    slot = jnp.arange(shape[2], dtype=jnp.int32) % BAND
    return (slot * stride + offset).astype(jnp.int32)


def block_scale(stream_key, extent, shards, smallest, largest):
    factor_of = 1.0
    for position, blocks in shards:
        draws = jax.random.uniform(jax.random.fold_in(jax.random.fold_in(stream_key, 6), position), (blocks,), jnp.float32, smallest / len(shards), largest / len(shards))
        factor_of = factor_of * jnp.repeat(jnp.exp(draws), extent[position] // blocks).reshape((-1,) + (1,) * (len(extent) - 1 - position))
    return factor_of


def scatter_about(own_key, shape, spread, reach, cuts=(), kind=jnp.bfloat16):
    array = spread * jax.random.normal(own_key, shape, jnp.float32)
    if cuts:
        array = array * block_scale(own_key, shape, cuts, -0.22, 0.18)
    return jnp.clip(array, -reach, reach).astype(kind)


def setup_inputs(seed: int = 0) -> dict:
    seeds = jax.random.split(jax.random.key(seed), 5)
    grads = draw_grads(jax.random.fold_in(seeds[4], 71), 0)
    momentum = scatter_about(seeds[1], (REPLICAS, ROWS, COLS), 1.0, 6.0, ((0, 64), (2, 4)), jnp.float32)
    master = scatter_about(seeds[2], (ROWS, COLS), 1.0, 6.0, ((1, 4),), jnp.float32)
    band_index = draw_band_index(jax.random.fold_in(seeds[4], 71), 0)
    return dict(grads=grads, momentum=momentum, master=master, band_index=band_index)


momentum_decay = 0.9
learn_rate = 0.05

def dct_table(order):
    freq = jnp.arange(order, dtype=jnp.float32)[:, None]
    place = jnp.arange(order, dtype=jnp.float32)[None, :]
    basis = jnp.cos(jnp.pi * (2.0 * place + 1.0) * freq / (2.0 * order))
    weight = jnp.where(freq == 0.0, jnp.sqrt(1.0 / order), jnp.sqrt(2.0 / order))
    return (basis * weight).astype(jnp.float32)

def forward(field, table):
    rows, cols = field.shape
    blocks = field.reshape(rows // BLOCK, BLOCK, cols // BLOCK, BLOCK)
    coeff = jnp.einsum('ka,racb,lb->rckl', table, blocks, table, precision=lax.Precision.HIGHEST)
    return coeff.reshape(rows // BLOCK, cols // BLOCK, BLOCK * BLOCK)

def inverse(coeff, table):
    rb, cb = (coeff.shape[0], coeff.shape[1])
    square = coeff.reshape(rb, cb, BLOCK, BLOCK)
    field = jnp.einsum('ka,rckl,lb->racb', table, square, table, precision=lax.Precision.HIGHEST)
    return field.reshape(rb * BLOCK, cb * BLOCK)

def scatter_band(band, index):
    rb, cb = (band.shape[0], band.shape[1])
    offsets = (jnp.arange(rb * cb, dtype=jnp.int32) * (BLOCK * BLOCK)).reshape(rb, cb, 1)
    places = (index + offsets).reshape(-1)
    flat = jnp.zeros((rb * cb * BLOCK * BLOCK,), jnp.float32).at[places].add(band.reshape(-1))
    return flat.reshape(rb, cb, BLOCK * BLOCK)

def reference(grads, momentum, master, band_index):
    table = dct_table(BLOCK)
    rb = ROWS // BLOCK
    cb = COLS // BLOCK

    def one_replica(total, item):
        grad_one, mom_one, index_one = item
        accumulated = momentum_decay * mom_one + grad_one.astype(jnp.float32)
        coeff = forward(accumulated, table)
        index = index_one.reshape(rb, cb, BAND).astype(jnp.int32)
        band = jnp.take_along_axis(coeff, index, axis=2)
        kept = scatter_band(band, index)
        fresh = accumulated - inverse(kept, table)
        return (total + kept, fresh)
    start = jnp.zeros((rb, cb, BLOCK * BLOCK), jnp.float32)
    total, new_momentum = lax.scan(one_replica, start, (grads, momentum, band_index))
    direction = inverse(total, table)
    shaped = direction.reshape(rb, BLOCK, cb, BLOCK)
    scale = jnp.sqrt(lax.optimization_barrier(jnp.mean(shaped * shaped, axis=(1, 3), keepdims=True)) + 1e-06)
    update = (shaped / (jnp.abs(shaped) + 0.1 * scale)).reshape(ROWS, COLS)
    weights_full = (master - learn_rate * update).astype(jnp.bfloat16)
    return (new_momentum, update, weights_full)
```

```python
import functools

import jax
import jax.numpy as jnp
import numpy as np
import ml_dtypes
from jax import lax
from jax.experimental import pallas as pl
from jax.experimental.pallas import tpu as pltpu
from jax.sharding import PartitionSpec as P

BLOCK = 64
BAND = 16
GROUP = 256
PER_STEP = 3

momentum_decay = 0.9
learn_rate = 0.05

bf16 = jnp.bfloat16
f32 = jnp.float32


def dct64():
    k = np.arange(BLOCK, dtype=np.float64)[:, None]
    n = np.arange(BLOCK, dtype=np.float64)[None, :]
    basis = np.cos(np.pi * (2.0 * n + 1.0) * k / (2.0 * BLOCK))
    return basis * np.where(k == 0.0, np.sqrt(1.0 / BLOCK), np.sqrt(2.0 / BLOCK))


def halves(table):
    hi = table.astype(np.float32).astype(ml_dtypes.bfloat16)
    lo = (table - hi.astype(np.float64)).astype(np.float32).astype(ml_dtypes.bfloat16)
    return hi, lo


def left_pair(table):
    hi, lo = halves(table)
    return np.concatenate([hi, hi], axis=1), lo


def make_tables():
    c = dct64()
    right = np.kron(np.eye(4), c.T)
    left = np.kron(np.eye(2), c)
    m, i = np.divmod(np.arange(BLOCK), 8)
    k1 = 4 * (m + 8 * (i // 4)) + i % 4
    back_perm = np.kron(np.eye(2), c[k1].T)
    spread = np.kron(np.eye(4), np.ones((BAND, BLOCK)))
    ones = np.kron(np.eye(4), np.ones((BLOCK, BLOCK)))
    as_bf16 = lambda a: a.astype(ml_dtypes.bfloat16)
    return dict(
        right=halves(right),
        right_t=halves(right.T),
        left=left_pair(left),
        left_t=left_pair(left.T),
        back=left_pair(back_perm),
        spread=as_bf16(spread),
        ones=as_bf16(ones),
    )


TABLES = make_tables()


def split(x):
    hi = x.astype(bf16)
    return hi, (x - hi.astype(f32)).astype(bf16)


def dot(a, b):
    return jnp.dot(a, b, preferred_element_type=f32)


def dot_nt(a, b):
    return lax.dot_general(a, b, (((1,), (1,)), ((), ())), preferred_element_type=f32)


def times_right(x, hi_ref, lo_ref):
    hi, lo = split(x)
    return dot(hi, hi_ref[...]) + (dot(lo, hi_ref[...]) + dot(hi, lo_ref[...]))


def times_left(pair_ref, lo_ref, x):
    hi, lo = split(x)
    return dot(pair_ref[...], jnp.concatenate([hi, lo], axis=0)) + dot(lo_ref[...], hi)


def local_kernel(
    own_ref, grads_ref, mom_ref, index_ref,
    r_hi, r_lo, rt_hi, rt_lo, l_pair, l_lo, lt_pair, lt_lo, spread_ref,
    fresh_ref, band_ref, wide,
):
    step = pl.program_id(0)
    groups = wide.shape[0]

    @pl.when(step == 0)
    def _():
        row = lax.broadcasted_iota(jnp.int32, (BLOCK, groups * BLOCK), 0)
        lane = lax.broadcasted_iota(jnp.int32, (BLOCK, groups * BLOCK), 1)
        mine = (lane & (BAND - 1)) == (row >> 2)
        for p in range(2):
            within = index_ref[0, p : p + 1, :] & 255
            placed = jnp.where(mine, jnp.broadcast_to(within, mine.shape), 0).astype(f32)
            for g in range(groups):
                wide[g, p * BLOCK : (p + 1) * BLOCK, :] = placed[:, g * BLOCK : (g + 1) * BLOCK].astype(bf16)

    row = lax.broadcasted_iota(jnp.int32, (2 * BLOCK, GROUP), 0)
    lane = lax.broadcasted_iota(jnp.int32, (2 * BLOCK, GROUP), 1)
    place = (((row & 3) << 6) + (lane & 63)).astype(f32)
    zrow = lax.broadcasted_iota(jnp.int32, (2 * BLOCK, BLOCK), 0)
    zlane = lax.broadcasted_iota(jnp.int32, (2 * BLOCK, BLOCK), 1)
    zmine = (zlane & (BAND - 1)) == ((zrow & 63) >> 2)
    for g in range(PER_STEP):
        cols = slice(g * GROUP, (g + 1) * GROUP)
        acc = momentum_decay * mom_ref[0, :, cols] + grads_ref[0, :, cols].astype(f32)
        coeff = times_left(l_pair, l_lo, times_right(acc, r_hi, r_lo))
        index = dot(wide[step * PER_STEP + g], spread_ref[...])
        kept = jnp.where(index == place, coeff, 0.0)
        hi, mid = split(kept)
        low = (kept - hi.astype(f32) - mid.astype(f32)).astype(bf16)
        sums = dot_nt(hi, spread_ref[...]) + (dot_nt(mid, spread_ref[...]) + dot_nt(low, spread_ref[...]))
        sums = jnp.where(zmine, sums, 0.0)
        top = jnp.sum(sums[:BLOCK], axis=0, keepdims=True)
        bottom = jnp.sum(sums[BLOCK:], axis=0, keepdims=True)
        band_ref[:, g * 128 : (g + 1) * 128] = jnp.concatenate([top, bottom], axis=1)
        back = times_left(lt_pair, lt_lo, times_right(kept, rt_hi, rt_lo))
        fresh_ref[0, :, cols] = acc - back


def full(shape):
    return pl.BlockSpec(shape, lambda *_: (0,) * len(shape))


def local_part(own, grads, momentum, band_index):
    cols = grads.shape[2]
    groups = cols // GROUP
    steps = groups // PER_STEP
    width = PER_STEP * GROUP
    t = TABLES
    consts = [*t["right"], *t["right_t"], *t["left"], *t["left_t"], t["spread"]]
    slab = pl.BlockSpec((1, 2 * BLOCK, width), lambda s, own: (0, 0, s))
    return pl.pallas_call(
        local_kernel,
        grid_spec=pltpu.PrefetchScalarGridSpec(
            num_scalar_prefetch=1,
            grid=(steps,),
            in_specs=[slab, slab, pl.BlockSpec((1, 2, band_index.shape[2]), lambda s, own: (own[0], 0, 0))]
            + [full(c.shape) for c in consts],
            out_specs=[slab, pl.BlockSpec((1, PER_STEP * 128), lambda s, own: (0, s))],
            scratch_shapes=[pltpu.VMEM((groups, 2 * BLOCK, BLOCK), bf16)],
        ),
        out_shape=[
            jax.ShapeDtypeStruct(grads.shape, f32),
            jax.ShapeDtypeStruct((1, groups * 128), f32),
        ],
        compiler_params=pltpu.CompilerParams(vmem_limit_bytes=32 * 2**20),
    )(own, grads, momentum, band_index, *[jnp.asarray(c) for c in consts])


def summed_coefficients(band, index):
    reps = band.shape[0]
    band_t = band.T
    within = index.T & 255
    half = jnp.where(lax.broadcasted_iota(jnp.int32, (8, 2 * reps), 1) >= reps, 4, 0)
    eight = lax.broadcasted_iota(jnp.int32, (8, 2 * reps), 0)
    k2_of = lax.broadcasted_iota(jnp.int32, (BLOCK, 2 * reps), 0)
    zero = jnp.zeros((8, 2 * reps), f32)
    quarter = lax.broadcasted_iota(jnp.int32, (16, GROUP), 1) >> 6
    parts = []
    for p in range(2):
        values, codes, places = [], [], []
        for q in range(4):
            base = p * 64 + q * 16
            join = lambda x: jnp.concatenate([x[base : base + 8], x[base + 8 : base + 16]], axis=1)
            w = join(within)
            values.append(join(band_t))
            codes.append((w >> 6) + half)
            places.append(w & 63)
        for t in range(4):
            his, los, hots = [], [], []
            for q in range(4):
                a, b = [], []
                for m in (2 * t, 2 * t + 1):
                    spread = lambda x: jnp.broadcast_to(x[m : m + 1], eight.shape)
                    a.append(jnp.where(spread(codes[q]) == eight, spread(values[q]), 0.0))
                    here = jnp.broadcast_to(places[q][m : m + 1], k2_of.shape) == k2_of
                    b.append(jnp.where(here, 1.0, 0.0).astype(bf16))
                left = jnp.concatenate(
                    [jnp.concatenate([a[0], zero], axis=1), jnp.concatenate([zero, a[1]], axis=1)], axis=0
                )
                hi, lo = split(left)
                his.append(hi)
                los.append(lo)
                hots.append(jnp.concatenate(b, axis=1))
            out = dot_nt(jnp.concatenate(his + los, axis=0), jnp.concatenate(hots, axis=0))
            out = out[:64] + out[64:]
            rows = jnp.where(quarter == 0, out[:16], 0.0)
            for q in range(1, 4):
                rows = jnp.where(quarter == q, out[16 * q : 16 * (q + 1)], rows)
            parts.append(rows)
    return jnp.concatenate(parts, axis=0)


def shared_group(band, index, master, rt_hi, rt_lo, b_pair, b_lo, ones_ref):
    total = summed_coefficients(band, index)
    direction = times_left(b_pair, b_lo, times_right(total, rt_hi, rt_lo))
    square = direction * direction
    sums = [
        jnp.broadcast_to(jnp.sum(square[p * BLOCK : (p + 1) * BLOCK], axis=0, keepdims=True), (8, GROUP))
        for p in range(2)
    ]
    hi, lo = split(jnp.concatenate(sums, axis=0))
    means = (dot(hi, ones_ref[...]) + dot(lo, ones_ref[...])) * (1.0 / (BLOCK * BLOCK))
    scale = 0.1 * jnp.sqrt(means + 1e-06)
    scale = jnp.concatenate(
        [jnp.broadcast_to(scale[8 * p : 8 * p + 1], (BLOCK, GROUP)) for p in range(2)], axis=0
    )
    update = direction / (jnp.abs(direction) + scale)
    return update, (master - learn_rate * update).astype(bf16)


def shared_kernel(band_ref, index_ref, master_ref, rt_hi, rt_lo, b_pair, b_lo, ones_ref, update_ref, weights_ref):
    for g in range(PER_STEP):
        lanes = slice(g * 128, (g + 1) * 128)
        cols = slice(g * GROUP, (g + 1) * GROUP)
        update, weights = shared_group(
            band_ref[:, lanes], index_ref[:, lanes], master_ref[:, cols], rt_hi, rt_lo, b_pair, b_lo, ones_ref
        )
        update_ref[:, cols] = update
        weights_ref[:, cols] = weights


def shared_part(bands, index, master):
    reps = bands.shape[0]
    rows, cols = master.shape
    steps = cols // (GROUP * PER_STEP)
    t = TABLES
    consts = [*t["right_t"], *t["back"], t["ones"]]
    slab = pl.BlockSpec((rows, PER_STEP * GROUP), lambda s: (0, s))
    lanes = pl.BlockSpec((reps, PER_STEP * 128), lambda s: (0, s))
    return pl.pallas_call(
        shared_kernel,
        grid=(steps,),
        in_specs=[lanes, lanes, slab] + [full(c.shape) for c in consts],
        out_specs=[slab, slab],
        out_shape=[jax.ShapeDtypeStruct(master.shape, f32), jax.ShapeDtypeStruct(master.shape, bf16)],
        compiler_params=pltpu.CompilerParams(vmem_limit_bytes=32 * 2**20),
    )(bands, index, master, *[jnp.asarray(c) for c in consts])


def by_group(band_index):
    reps, _, lanes = band_index.shape
    split_up = band_index.reshape(reps, 2, lanes // BLOCK, BLOCK)
    return split_up.transpose(0, 2, 1, 3).reshape(reps, 2 * lanes)


def shards(grads, momentum, master, band_index):
    own = lax.axis_index("rep").astype(jnp.int32)[None]
    fresh, band = local_part(own, grads, momentum, band_index)
    bands = lax.all_gather(band, "rep", axis=0, tiled=True)
    update, weights_local = shared_part(bands, by_group(band_index), master)
    weights_full = lax.all_gather(weights_local, "fsdp", axis=1, tiled=True)
    return (fresh, update, weights_full)


def solution(mesh):
    in_specs = (
        P("rep", None, "fsdp"),
        P("rep", None, "fsdp"),
        P(None, "fsdp"),
        P(None, None, "fsdp"),
    )
    out_specs = (P("rep", None, "fsdp"), P(None, "fsdp"), P())
    return jax.shard_map(shards, mesh=mesh, in_specs=in_specs, out_specs=out_specs, check_vma=False)
```

```python
import functools

import jax
import jax.numpy as jnp
import numpy as np
import ml_dtypes
from jax import lax
from jax.experimental import pallas as pl
from jax.experimental.pallas import tpu as pltpu
from jax.sharding import PartitionSpec as P

BLOCK = 64
BAND = 16
GROUP = 256
PER_STEP = 3

momentum_decay = 0.9
learn_rate = 0.05

bf16 = jnp.bfloat16
f32 = jnp.float32
MESH = pl.DeviceIdType.MESH


def dct64():
    k = np.arange(BLOCK, dtype=np.float64)[:, None]
    n = np.arange(BLOCK, dtype=np.float64)[None, :]
    basis = np.cos(np.pi * (2.0 * n + 1.0) * k / (2.0 * BLOCK))
    return basis * np.where(k == 0.0, np.sqrt(1.0 / BLOCK), np.sqrt(2.0 / BLOCK))


def halves(table):
    hi = table.astype(np.float32).astype(ml_dtypes.bfloat16)
    lo = (table - hi.astype(np.float64)).astype(np.float32).astype(ml_dtypes.bfloat16)
    return hi, lo


def left_pair(table):
    hi, lo = halves(table)
    return np.concatenate([hi, hi], axis=1), lo


def make_tables():
    c = dct64()
    right = np.kron(np.eye(4), c.T)
    left = np.kron(np.eye(2), c)
    m, i = np.divmod(np.arange(BLOCK), 8)
    k1 = 4 * (m + 8 * (i // 4)) + i % 4
    back_perm = np.kron(np.eye(2), c[k1].T)
    spread = np.kron(np.eye(4), np.ones((BAND, BLOCK)))
    ones = np.kron(np.eye(4), np.ones((BLOCK, BLOCK)))
    as_bf16 = lambda a: a.astype(ml_dtypes.bfloat16)
    return dict(
        right=halves(right),
        right_t=halves(right.T),
        left=left_pair(left),
        left_t=left_pair(left.T),
        back=left_pair(back_perm),
        spread=as_bf16(spread),
        ones=as_bf16(ones),
    )


TABLES = make_tables()


def split(x):
    hi = x.astype(bf16)
    return hi, (x - hi.astype(f32)).astype(bf16)


def dot(a, b):
    return jnp.dot(a, b, preferred_element_type=f32)


def dot_nt(a, b):
    return lax.dot_general(a, b, (((1,), (1,)), ((), ())), preferred_element_type=f32)


def times_right(x, hi_ref, lo_ref):
    hi, lo = split(x)
    return dot(hi, hi_ref[...]) + (dot(lo, hi_ref[...]) + dot(hi, lo_ref[...]))


def times_left(pair_ref, lo_ref, x):
    hi, lo = split(x)
    return dot(pair_ref[...], jnp.concatenate([hi, lo], axis=0)) + dot(lo_ref[...], hi)


def local_kernel(
    own_ref, grads_ref, mom_ref, index_ref,
    r_hi, r_lo, rt_hi, rt_lo, l_pair, l_lo, lt_pair, lt_lo, spread_ref,
    fresh_ref, band_ref, wide,
):
    step = pl.program_id(0)
    groups = wide.shape[0]

    @pl.when(step == 0)
    def _():
        row = lax.broadcasted_iota(jnp.int32, (BLOCK, groups * BLOCK), 0)
        lane = lax.broadcasted_iota(jnp.int32, (BLOCK, groups * BLOCK), 1)
        mine = (lane & (BAND - 1)) == (row >> 2)
        for p in range(2):
            within = index_ref[0, p : p + 1, :] & 255
            placed = jnp.where(mine, jnp.broadcast_to(within, mine.shape), 0).astype(f32)
            for g in range(groups):
                wide[g, p * BLOCK : (p + 1) * BLOCK, :] = placed[:, g * BLOCK : (g + 1) * BLOCK].astype(bf16)

    row = lax.broadcasted_iota(jnp.int32, (2 * BLOCK, GROUP), 0)
    lane = lax.broadcasted_iota(jnp.int32, (2 * BLOCK, GROUP), 1)
    place = (((row & 3) << 6) + (lane & 63)).astype(f32)
    zrow = lax.broadcasted_iota(jnp.int32, (2 * BLOCK, BLOCK), 0)
    zlane = lax.broadcasted_iota(jnp.int32, (2 * BLOCK, BLOCK), 1)
    zmine = (zlane & (BAND - 1)) == ((zrow & 63) >> 2)
    for g in range(PER_STEP):
        cols = slice(g * GROUP, (g + 1) * GROUP)
        acc = momentum_decay * mom_ref[0, :, cols] + grads_ref[0, :, cols].astype(f32)
        coeff = times_left(l_pair, l_lo, times_right(acc, r_hi, r_lo))
        index = dot(wide[step * PER_STEP + g], spread_ref[...])
        kept = jnp.where(index == place, coeff, 0.0)
        hi, mid = split(kept)
        low = (kept - hi.astype(f32) - mid.astype(f32)).astype(bf16)
        sums = dot_nt(hi, spread_ref[...]) + (dot_nt(mid, spread_ref[...]) + dot_nt(low, spread_ref[...]))
        sums = jnp.where(zmine, sums, 0.0)
        top = jnp.sum(sums[:BLOCK], axis=0, keepdims=True)
        bottom = jnp.sum(sums[BLOCK:], axis=0, keepdims=True)
        band_ref[pl.ds(step * PER_STEP + g, 1), :] = jnp.concatenate([top, bottom], axis=1)
        back = times_left(lt_pair, lt_lo, times_right(kept, rt_hi, rt_lo))
        fresh_ref[0, :, cols] = acc - back


def full(shape):
    return pl.BlockSpec(shape, lambda *_: (0,) * len(shape))


def local_part(own, grads, momentum, band_index):
    cols = grads.shape[2]
    groups = cols // GROUP
    steps = groups // PER_STEP
    width = PER_STEP * GROUP
    t = TABLES
    consts = [*t["right"], *t["right_t"], *t["left"], *t["left_t"], t["spread"]]
    slab = pl.BlockSpec((1, 2 * BLOCK, width), lambda s, own: (0, 0, s))
    return pl.pallas_call(
        local_kernel,
        grid_spec=pltpu.PrefetchScalarGridSpec(
            num_scalar_prefetch=1,
            grid=(steps,),
            in_specs=[slab, slab, pl.BlockSpec((1, 2, band_index.shape[2]), lambda s, own: (own[0], 0, 0))]
            + [full(c.shape) for c in consts],
            out_specs=[slab, full((groups, 128))],
            scratch_shapes=[pltpu.VMEM((groups, 2 * BLOCK, BLOCK), bf16)],
        ),
        out_shape=[
            jax.ShapeDtypeStruct(grads.shape, f32),
            jax.ShapeDtypeStruct((groups, 128), f32),
        ],
        compiler_params=pltpu.CompilerParams(vmem_limit_bytes=32 * 2**20),
    )(own, grads, momentum, band_index, *[jnp.asarray(c) for c in consts])


def summed_coefficients(band, index):
    reps = band.shape[1] // 2
    half = jnp.where(lax.broadcasted_iota(jnp.int32, (8, 2 * reps), 1) >= reps, 4, 0)
    eight = lax.broadcasted_iota(jnp.int32, (8, 2 * reps), 0)
    k2_of = lax.broadcasted_iota(jnp.int32, (BLOCK, 2 * reps), 0)
    zero = jnp.zeros((8, 2 * reps), f32)
    quarter = lax.broadcasted_iota(jnp.int32, (16, GROUP), 1) >> 6
    parts = []
    for p in range(2):
        values, codes, places = [], [], []
        for q in range(4):
            base = (p * 4 + q) * 8
            w = index[base : base + 8]
            values.append(band[base : base + 8])
            codes.append((w >> 6) + half)
            places.append(w & 63)
        for t in range(4):
            his, los, hots = [], [], []
            for q in range(4):
                a, b = [], []
                for m in (2 * t, 2 * t + 1):
                    spread = lambda x: jnp.broadcast_to(x[m : m + 1], eight.shape)
                    a.append(jnp.where(spread(codes[q]) == eight, spread(values[q]), 0.0))
                    here = jnp.broadcast_to(places[q][m : m + 1], k2_of.shape) == k2_of
                    b.append(jnp.where(here, 1.0, 0.0).astype(bf16))
                left = jnp.concatenate(
                    [jnp.concatenate([a[0], zero], axis=1), jnp.concatenate([zero, a[1]], axis=1)], axis=0
                )
                hi, lo = split(left)
                his.append(hi)
                los.append(lo)
                hots.append(jnp.concatenate(b, axis=1))
            out = dot_nt(jnp.concatenate(his + los, axis=0), jnp.concatenate(hots, axis=0))
            out = out[:64] + out[64:]
            rows = jnp.where(quarter == 0, out[:16], 0.0)
            for q in range(1, 4):
                rows = jnp.where(quarter == q, out[16 * q : 16 * (q + 1)], rows)
            parts.append(rows)
    return jnp.concatenate(parts, axis=0)


def shared_group(band, index, master, rt_hi, rt_lo, b_pair, b_lo, ones_ref):
    total = summed_coefficients(band, index)
    direction = times_left(b_pair, b_lo, times_right(total, rt_hi, rt_lo))
    square = direction * direction
    sums = [
        jnp.broadcast_to(jnp.sum(square[p * BLOCK : (p + 1) * BLOCK], axis=0, keepdims=True), (8, GROUP))
        for p in range(2)
    ]
    hi, lo = split(jnp.concatenate(sums, axis=0))
    means = (dot(hi, ones_ref[...]) + dot(lo, ones_ref[...])) * (1.0 / (BLOCK * BLOCK))
    scale = 0.1 * jnp.sqrt(means + 1e-06)
    scale = jnp.concatenate(
        [jnp.broadcast_to(scale[8 * p : 8 * p + 1], (BLOCK, GROUP)) for p in range(2)], axis=0
    )
    update = direction / (jnp.abs(direction) + scale)
    return update, (master - learn_rate * update).astype(bf16)


def shared_kernel(band_ref, index_ref, master_ref, rt_hi, rt_lo, b_pair, b_lo, ones_ref, update_ref, weights_ref):
    for g in range(PER_STEP):
        lanes = slice(g * 64, (g + 1) * 64)
        cols = slice(g * GROUP, (g + 1) * GROUP)
        update, weights = shared_group(
            band_ref[lanes, :], index_ref[lanes, :], master_ref[:, cols], rt_hi, rt_lo, b_pair, b_lo, ones_ref
        )
        update_ref[:, cols] = update
        weights_ref[:, cols] = weights


def shared_part(bands, index, master):
    rows, cols = master.shape
    steps = cols // (GROUP * PER_STEP)
    t = TABLES
    consts = [*t["right_t"], *t["back"], t["ones"]]
    slab = pl.BlockSpec((rows, PER_STEP * GROUP), lambda s: (0, s))
    lanes = pl.BlockSpec((PER_STEP * 64, 128), lambda s: (s, 0))
    return pl.pallas_call(
        shared_kernel,
        grid=(steps,),
        in_specs=[lanes, lanes, slab] + [full(c.shape) for c in consts],
        out_specs=[slab, slab],
        out_shape=[jax.ShapeDtypeStruct(master.shape, f32), jax.ShapeDtypeStruct(master.shape, bf16)],
        compiler_params=pltpu.CompilerParams(vmem_limit_bytes=32 * 2**20),
    )(bands, index, master, *[jnp.asarray(c) for c in consts])


def rep_parts(r):
    return r // 16, (r // 2) % 8, r % 2


def rep_of(x, z, core):
    return x * 16 + z * 2 + core


def gather_kernel(
    band_ref, index_ref, band_out, index_out, rows, index_rows,
    own_sem, index_sem, z_send, z_recv, x_send, x_recv, s_send, s_recv,
):
    x, z, core = rep_parts(lax.axis_index("rep"))
    groups = rows.shape[1]
    other = 1 - core
    z_peers = [rep_of(x, lax.rem(z + d, 8), core) for d in range(1, 8)]
    x_peers = [rep_of(lax.rem(x + d, 4), z, core) for d in range(1, 4)]
    sibling = rep_of(x, z, other)

    mine = core * 32 + x * 8 + z
    own = pltpu.make_async_copy(band_ref, rows.at[mine], own_sem)
    own.start()
    pulls = []
    for c in range(2):
        pull = pltpu.make_async_copy(index_ref.at[:, :, c], index_rows.at[c], index_sem.at[c])
        pull.start()
        pulls.append(pull)

    barrier = pltpu.get_barrier_semaphore()
    for peer in z_peers + x_peers + [sibling]:
        pl.semaphore_signal(barrier, inc=1, device_id={"rep": peer}, device_id_type=MESH)
    pl.semaphore_wait(barrier, 11)
    own.wait()

    def remote(ref, send, recv, peer):
        return pltpu.make_async_remote_copy(
            src_ref=ref, dst_ref=ref, send_sem=send, recv_sem=recv,
            device_id={"rep": peer}, device_id_type=MESH,
        )

    z_copies = [remote(rows.at[mine], z_send.at[d], z_recv.at[d], peer) for d, peer in enumerate(z_peers)]
    for copy in z_copies:
        copy.start()

    for pull in pulls:
        pull.wait()
    for p in range(2):
        for k in range((groups + 1) // 2):
            lanes = min(128, groups * BLOCK - k * 128)
            chunk = index_rows[:, :, :, p, k * 128 : k * 128 + lanes].reshape(64, lanes)
            turned = chunk.T & 255
            for b in range(lanes // BAND):
                g = 2 * k + b // 4
                at = ((g * 2 + p) * 4 + b % 4) * 8
                index_out[at : at + 8, :] = jnp.concatenate(
                    [turned[b * 16 : b * 16 + 8], turned[b * 16 + 8 : b * 16 + 16]], axis=1
                )

    for copy in z_copies:
        copy.wait()
    bundle = rows.at[pl.ds(core * 32 + x * 8, 8)]
    x_copies = [remote(bundle, x_send.at[d], x_recv.at[d], peer) for d, peer in enumerate(x_peers)]
    for copy in x_copies:
        copy.start()
    s_copies = [remote(bundle, s_send.at[0], s_recv.at[0], sibling)]
    s_copies[0].start()
    for d in range(1, 4):
        x_copies[d - 1].wait_recv()
        source = lax.rem(x + 4 - d, 4)
        part = rows.at[pl.ds(core * 32 + source * 8, 8)]
        copy = remote(part, s_send.at[d], s_recv.at[d], sibling)
        copy.start()
        s_copies.append(copy)
    for copy in x_copies:
        copy.wait_send()
    for copy in s_copies:
        copy.wait()

    @pl.loop(0, groups)
    def _(g):
        turned = rows[:, g, :].T
        for b in range(8):
            band_out[pl.ds(pl.multiple_of(g * 64 + b * 8, 8), 8), :] = jnp.concatenate(
                [turned[b * 16 : b * 16 + 8], turned[b * 16 + 8 : b * 16 + 16]], axis=1
            )


def gather_part(band, band_index):
    groups = band.shape[0]
    reps, _, lanes = band_index.shape
    dma = pltpu.SemaphoreType.DMA
    shape = (groups * 64, 128)
    return pl.pallas_call(
        gather_kernel,
        in_specs=[pl.BlockSpec(memory_space=pl.ANY)] * 2,
        out_specs=[pl.BlockSpec(memory_space=pltpu.VMEM)] * 2,
        out_shape=[jax.ShapeDtypeStruct(shape, f32), jax.ShapeDtypeStruct(shape, jnp.int32)],
        scratch_shapes=[
            pltpu.VMEM((reps, groups, 128), f32),
            pltpu.VMEM((2, 4, 8, 2, lanes), jnp.int32),
            dma, dma((2,)), dma((7,)), dma((7,)), dma((3,)), dma((3,)), dma((4,)), dma((4,)),
        ],
        compiler_params=pltpu.CompilerParams(
            collective_id=0, has_side_effects=True, vmem_limit_bytes=32 * 2**20
        ),
    )(band, band_index.reshape(4, 8, 2, 2, lanes))


def shards(grads, momentum, master, band_index):
    own = lax.axis_index("rep").astype(jnp.int32)[None]
    fresh, band = local_part(own, grads, momentum, band_index)
    bands, index = gather_part(band, band_index)
    update, weights_local = shared_part(bands, index, master)
    weights_full = lax.all_gather(weights_local, "fsdp", axis=1, tiled=True)
    return (fresh, update, weights_full)


def solution(mesh):
    in_specs = (
        P("rep", None, "fsdp"),
        P("rep", None, "fsdp"),
        P(None, "fsdp"),
        P(None, None, "fsdp"),
    )
    out_specs = (P("rep", None, "fsdp"), P(None, "fsdp"), P())
    return jax.shard_map(shards, mesh=mesh, in_specs=in_specs, out_specs=out_specs, check_vma=False)
```

```python
import functools

import jax
import jax.numpy as jnp
import numpy as np
import ml_dtypes
from jax import lax
from jax.experimental import pallas as pl
from jax.experimental.pallas import tpu as pltpu
from jax.sharding import PartitionSpec as P

BLOCK = 64
BAND = 16
GROUP = 256
PER_STEP = 3

momentum_decay = 0.9
learn_rate = 0.05

bf16 = jnp.bfloat16
f32 = jnp.float32
MESH = pl.DeviceIdType.MESH
VMEM_LIMIT = 60 * 2**20


def dct64():
    k = np.arange(BLOCK, dtype=np.float64)[:, None]
    n = np.arange(BLOCK, dtype=np.float64)[None, :]
    basis = np.cos(np.pi * (2.0 * n + 1.0) * k / (2.0 * BLOCK))
    return basis * np.where(k == 0.0, np.sqrt(1.0 / BLOCK), np.sqrt(2.0 / BLOCK))


def halves(table):
    hi = table.astype(np.float32).astype(ml_dtypes.bfloat16)
    lo = (table - hi.astype(np.float64)).astype(np.float32).astype(ml_dtypes.bfloat16)
    return hi, lo


def left_pair(table):
    hi, lo = halves(table)
    return np.concatenate([hi, hi], axis=1), lo


def make_tables():
    c = dct64()
    right = np.kron(np.eye(4), c.T)
    left = np.kron(np.eye(2), c)
    m, i = np.divmod(np.arange(BLOCK), 8)
    k1 = 4 * (m + 8 * (i // 4)) + i % 4
    back_perm = np.kron(np.eye(2), c[k1].T)
    spread = np.kron(np.eye(4), np.ones((BAND, BLOCK)))
    ones = np.kron(np.eye(4), np.ones((BLOCK, BLOCK)))
    as_bf16 = lambda a: a.astype(ml_dtypes.bfloat16)
    return dict(
        right=halves(right),
        right_t=halves(right.T),
        left=left_pair(left),
        left_t=left_pair(left.T),
        back=left_pair(back_perm),
        spread=as_bf16(spread),
        ones=as_bf16(ones),
    )


TABLES = make_tables()


def split(x):
    hi = x.astype(bf16)
    return hi, (x - hi.astype(f32)).astype(bf16)


def dot(a, b):
    return jnp.dot(a, b, preferred_element_type=f32)


def dot_nt(a, b):
    return lax.dot_general(a, b, (((1,), (1,)), ((), ())), preferred_element_type=f32)


def times_right(x, hi_ref, lo_ref):
    hi, lo = split(x)
    return dot(hi, hi_ref[...]) + (dot(lo, hi_ref[...]) + dot(hi, lo_ref[...]))


def times_left(pair_ref, lo_ref, x):
    hi, lo = split(x)
    return dot(pair_ref[...], jnp.concatenate([hi, lo], axis=0)) + dot(lo_ref[...], hi)


def local_kernel(
    own_ref, grads_ref, mom_ref, index_ref, table_ref, fresh_ref, band_ref, wide,
):
    r_hi, r_lo, rt_hi, rt_lo = (table_ref.at[k * 256 : (k + 1) * 256] for k in range(4))
    l_pair, lt_pair = (table_ref.at[1024 + k * 128 : 1152 + k * 128] for k in range(2))
    l_lo, lt_lo = (table_ref.at[1280:1408, k * 128 : (k + 1) * 128] for k in range(2))
    spread_ref = table_ref.at[1408:1472]
    step = pl.program_id(0)
    groups = wide.shape[0]

    @pl.when(step == 0)
    def _():
        row = lax.broadcasted_iota(jnp.int32, (BLOCK, groups * BLOCK), 0)
        lane = lax.broadcasted_iota(jnp.int32, (BLOCK, groups * BLOCK), 1)
        mine = (lane & (BAND - 1)) == (row >> 2)
        for p in range(2):
            within = index_ref[0, p : p + 1, :] & 255
            placed = jnp.where(mine, jnp.broadcast_to(within, mine.shape), 0).astype(f32)
            for g in range(groups):
                wide[g, p * BLOCK : (p + 1) * BLOCK, :] = placed[:, g * BLOCK : (g + 1) * BLOCK].astype(bf16)

    row = lax.broadcasted_iota(jnp.int32, (2 * BLOCK, GROUP), 0)
    lane = lax.broadcasted_iota(jnp.int32, (2 * BLOCK, GROUP), 1)
    place = (((row & 3) << 6) + (lane & 63)).astype(f32)
    zrow = lax.broadcasted_iota(jnp.int32, (2 * BLOCK, BLOCK), 0)
    zlane = lax.broadcasted_iota(jnp.int32, (2 * BLOCK, BLOCK), 1)
    zmine = (zlane & (BAND - 1)) == ((zrow & 63) >> 2)
    for g in range(PER_STEP):
        cols = slice(g * GROUP, (g + 1) * GROUP)
        acc = momentum_decay * mom_ref[0, :, cols] + grads_ref[0, :, cols].astype(f32)
        coeff = times_left(l_pair, l_lo, times_right(acc, r_hi, r_lo))
        index = dot(wide[step * PER_STEP + g], spread_ref[...])
        kept = jnp.where(index == place, coeff, 0.0)
        hi, mid = split(kept)
        low = (kept - hi.astype(f32) - mid.astype(f32)).astype(bf16)
        sums = dot_nt(hi, spread_ref[...]) + (dot_nt(mid, spread_ref[...]) + dot_nt(low, spread_ref[...]))
        sums = jnp.where(zmine, sums, 0.0)
        top = jnp.sum(sums[:BLOCK], axis=0, keepdims=True)
        bottom = jnp.sum(sums[BLOCK:], axis=0, keepdims=True)
        band_ref[pl.ds(step * PER_STEP + g, 1), :] = jnp.concatenate([top, bottom], axis=1)
        back = times_left(lt_pair, lt_lo, times_right(kept, rt_hi, rt_lo))
        fresh_ref[0, :, cols] = acc - back


def full(shape):
    return pl.BlockSpec(shape, lambda *_: (0,) * len(shape))


def local_part(own, grads, momentum, band_index):
    cols = grads.shape[2]
    groups = cols // GROUP
    steps = groups // PER_STEP
    width = PER_STEP * GROUP
    t = TABLES
    lows = np.concatenate([t["left"][1], t["left_t"][1]], axis=1)
    table = np.concatenate(
        [*t["right"], *t["right_t"], t["left"][0], t["left_t"][0], lows, t["spread"]], axis=0
    )
    slab = pl.BlockSpec((1, 2 * BLOCK, width), lambda s, own: (0, 0, s))
    return pl.pallas_call(
        local_kernel,
        grid_spec=pltpu.PrefetchScalarGridSpec(
            num_scalar_prefetch=1,
            grid=(steps,),
            in_specs=[slab, slab, pl.BlockSpec((1, 2, band_index.shape[2]), lambda s, own: (own[0], 0, 0))]
            + [full(table.shape)],
            out_specs=[slab, full((groups, 128))],
            scratch_shapes=[pltpu.VMEM((groups, 2 * BLOCK, BLOCK), bf16)],
        ),
        out_shape=[
            jax.ShapeDtypeStruct(grads.shape, f32),
            jax.ShapeDtypeStruct((groups, 128), f32),
        ],
        compiler_params=pltpu.CompilerParams(vmem_limit_bytes=VMEM_LIMIT),
    )(own, grads, momentum, band_index, jnp.asarray(table))


def summed_coefficients(band, index):
    reps = band.shape[1] // 2
    half = jnp.where(lax.broadcasted_iota(jnp.int32, (8, 2 * reps), 1) >= reps, 4, 0)
    eight = lax.broadcasted_iota(jnp.int32, (8, 2 * reps), 0)
    k2_of = lax.broadcasted_iota(jnp.int32, (BLOCK, 2 * reps), 0)
    zero = jnp.zeros((8, 2 * reps), f32)
    quarter = lax.broadcasted_iota(jnp.int32, (16, GROUP), 1) >> 6
    parts = []
    for p in range(2):
        values, codes, places = [], [], []
        for q in range(4):
            base = (p * 4 + q) * 8
            w = index[base : base + 8]
            values.append(band[base : base + 8])
            codes.append((w >> 6) + half)
            places.append(w & 63)
        for t in range(4):
            his, los, hots = [], [], []
            for q in range(4):
                a, b = [], []
                for m in (2 * t, 2 * t + 1):
                    spread = lambda x: jnp.broadcast_to(x[m : m + 1], eight.shape)
                    a.append(jnp.where(spread(codes[q]) == eight, spread(values[q]), 0.0))
                    here = jnp.broadcast_to(places[q][m : m + 1], k2_of.shape) == k2_of
                    b.append(jnp.where(here, 1.0, 0.0).astype(bf16))
                left = jnp.concatenate(
                    [jnp.concatenate([a[0], zero], axis=1), jnp.concatenate([zero, a[1]], axis=1)], axis=0
                )
                hi, lo = split(left)
                his.append(hi)
                los.append(lo)
                hots.append(jnp.concatenate(b, axis=1))
            out = dot_nt(jnp.concatenate(his + los, axis=0), jnp.concatenate(hots, axis=0))
            out = out[:64] + out[64:]
            rows = jnp.where(quarter == 0, out[:16], 0.0)
            for q in range(1, 4):
                rows = jnp.where(quarter == q, out[16 * q : 16 * (q + 1)], rows)
            parts.append(rows)
    return jnp.concatenate(parts, axis=0)


def shared_group(band, index, master, rt_hi, rt_lo, b_pair, b_lo, ones_ref):
    total = summed_coefficients(band, index)
    direction = times_left(b_pair, b_lo, times_right(total, rt_hi, rt_lo))
    square = direction * direction
    sums = [
        jnp.broadcast_to(jnp.sum(square[p * BLOCK : (p + 1) * BLOCK], axis=0, keepdims=True), (8, GROUP))
        for p in range(2)
    ]
    hi, lo = split(jnp.concatenate(sums, axis=0))
    means = (dot(hi, ones_ref[...]) + dot(lo, ones_ref[...])) * (1.0 / (BLOCK * BLOCK))
    scale = 0.1 * jnp.sqrt(means + 1e-06)
    scale = jnp.concatenate(
        [jnp.broadcast_to(scale[8 * p : 8 * p + 1], (BLOCK, GROUP)) for p in range(2)], axis=0
    )
    update = direction / (jnp.abs(direction) + scale)
    return update, (master - learn_rate * update).astype(bf16)


def shared_table_array():
    t = TABLES
    pair, low = t["back"]
    low = np.concatenate([low, np.zeros_like(low)], axis=1)
    return jnp.asarray(np.concatenate([*t["right_t"], t["ones"], pair, low], axis=0))


def shared_tables(ref):
    return ref.at[0:256], ref.at[256:512], ref.at[768:896], ref.at[896:1024, 0:128], ref.at[512:768]


def rep_parts(r):
    return r // 16, (r // 2) % 8, r % 2


def rep_of(x, z, core):
    return x * 16 + z * 2 + core


def gather_kernel(
    band_ref, index_ref, band_out, index_out, rows, index_rows,
    own_sem, index_sem, z_send, z_recv, x_send, x_recv, s_send, s_recv,
):
    x, z, core = rep_parts(lax.axis_index("rep"))
    groups = rows.shape[1]
    other = 1 - core
    z_peers = [rep_of(x, lax.rem(z + d, 8), core) for d in range(1, 8)]
    x_peers = [rep_of(lax.rem(x + d, 4), z, core) for d in range(1, 4)]
    sibling = rep_of(x, z, other)

    mine = core * 32 + x * 8 + z
    own = pltpu.make_async_copy(band_ref, rows.at[mine], own_sem)
    own.start()
    pulls = []
    for c in range(2):
        pull = pltpu.make_async_copy(index_ref.at[:, :, c], index_rows.at[c], index_sem.at[c])
        pull.start()
        pulls.append(pull)

    barrier = pltpu.get_barrier_semaphore()
    for peer in z_peers + x_peers + [sibling]:
        pl.semaphore_signal(barrier, inc=1, device_id={"rep": peer}, device_id_type=MESH)
    pl.semaphore_wait(barrier, 11)
    own.wait()

    def remote(ref, send, recv, peer):
        return pltpu.make_async_remote_copy(
            src_ref=ref, dst_ref=ref, send_sem=send, recv_sem=recv,
            device_id={"rep": peer}, device_id_type=MESH,
        )

    z_copies = [remote(rows.at[mine], z_send.at[d], z_recv.at[d], peer) for d, peer in enumerate(z_peers)]
    for copy in z_copies:
        copy.start()

    for pull in pulls:
        pull.wait()
    for p in range(2):
        for k in range((groups + 1) // 2):
            lanes = min(128, groups * BLOCK - k * 128)
            chunk = index_rows[:, :, :, p, k * 128 : k * 128 + lanes].reshape(64, lanes)
            turned = chunk.T & 255
            for b in range(lanes // BAND):
                g = 2 * k + b // 4
                at = ((g * 2 + p) * 4 + b % 4) * 8
                index_out[at : at + 8, :] = jnp.concatenate(
                    [turned[b * 16 : b * 16 + 8], turned[b * 16 + 8 : b * 16 + 16]], axis=1
                )

    for copy in z_copies:
        copy.wait()
    bundle = rows.at[pl.ds(core * 32 + x * 8, 8)]
    x_copies = [remote(bundle, x_send.at[d], x_recv.at[d], peer) for d, peer in enumerate(x_peers)]
    for copy in x_copies:
        copy.start()
    s_copies = [remote(bundle, s_send.at[0], s_recv.at[0], sibling)]
    s_copies[0].start()
    for d in range(1, 4):
        x_copies[d - 1].wait_recv()
        source = lax.rem(x + 4 - d, 4)
        part = rows.at[pl.ds(core * 32 + source * 8, 8)]
        copy = remote(part, s_send.at[d], s_recv.at[d], sibling)
        copy.start()
        s_copies.append(copy)
    for copy in x_copies:
        copy.wait_send()
    for copy in s_copies:
        copy.wait()

    @pl.loop(0, groups)
    def _(g):
        turned = rows[:, g, :].T
        for b in range(8):
            band_out[pl.ds(pl.multiple_of(g * 64 + b * 8, 8), 8), :] = jnp.concatenate(
                [turned[b * 16 : b * 16 + 8], turned[b * 16 + 8 : b * 16 + 16]], axis=1
            )


def gather_part(band, band_index):
    groups = band.shape[0]
    reps, _, lanes = band_index.shape
    dma = pltpu.SemaphoreType.DMA
    shape = (groups * 64, 128)
    return pl.pallas_call(
        gather_kernel,
        in_specs=[pl.BlockSpec(memory_space=pl.ANY)] * 2,
        out_specs=[pl.BlockSpec(memory_space=pltpu.VMEM)] * 2,
        out_shape=[jax.ShapeDtypeStruct(shape, f32), jax.ShapeDtypeStruct(shape, jnp.int32)],
        scratch_shapes=[
            pltpu.VMEM((reps, groups, 128), f32),
            pltpu.VMEM((2, 4, 8, 2, lanes), jnp.int32),
            dma, dma((2,)), dma((7,)), dma((7,)), dma((3,)), dma((3,)), dma((4,)), dma((4,)),
        ],
        compiler_params=pltpu.CompilerParams(
            collective_id=0, has_side_effects=True, vmem_limit_bytes=VMEM_LIMIT
        ),
    )(band, band_index.reshape(4, 8, 2, 2, lanes))


UNITS = 7
WIDE = 2 * GROUP
DIRECT = 64


def update_kernel(
    band_ref, index_ref, master_ref, table_ref, update_out, weights_out,
    masters, updates, slots,
    m_sem, y_send, y_recv, x_send, x_recv, s_send, s_recv, o_sem, t_sem,
):
    rep = lax.axis_index("rep")
    shard = lax.axis_index("fsdp")
    x, z, core = rep_parts(rep)
    cols = masters.shape[1]
    groups = cols // GROUP
    sibling = rep_of(x, z, 1 - core)
    y_peers = [lax.rem(shard + d, 4) for d in range(1, 4)]
    x_peers = [rep_of(lax.rem(x + d, 4), z, core) for d in range(1, 4)]
    share = (2 * BLOCK - DIRECT) // 4

    def first_group(of_core, unit):
        return 2 * unit + of_core * (groups - 2 - 4 * unit)

    def span(of_core, unit):
        return pl.ds(pl.multiple_of(first_group(of_core, unit) * GROUP, GROUP), WIDE)

    def last_span(of_core):
        start = (groups // 2 - 1 + 2 * of_core) * GROUP
        return pl.ds(pl.multiple_of(start, GROUP), GROUP)

    def master_copy(unit):
        at = span(core, unit)
        return pltpu.make_async_copy(master_ref.at[:, at], masters.at[:, at], m_sem.at[unit])

    def share_rows(of_x):
        return pl.ds(pl.multiple_of(DIRECT + of_x * share, 16), share)

    def y_copies(unit):
        at = span(core, unit)
        out = []
        for d in range(3):
            for k, rows in enumerate((pl.ds(0, DIRECT), share_rows(x))):
                out.append(pltpu.make_async_remote_copy(
                    src_ref=slots.at[0, rows, at], dst_ref=slots.at[d + 1, rows, at],
                    send_sem=y_send.at[unit, d, k], recv_sem=y_recv.at[unit, d, k],
                    device_id={"fsdp": y_peers[d]}, device_id_type=MESH,
                ))
        return out

    def x_copies(unit, arriving):
        at = span(core, unit)
        out = []
        for d in range(3):
            rows = share_rows(lax.rem(x + 3 - d, 4) if arriving else x)
            part = slots.at[pl.ds(1, 3), rows, at]
            out.append(pltpu.make_async_remote_copy(
                src_ref=part, dst_ref=part, send_sem=x_send.at[unit, d], recv_sem=x_recv.at[unit, d],
                device_id={"rep": x_peers[d]}, device_id_type=MESH,
            ))
        return out

    def s_copies(unit, at):
        return [
            pltpu.make_async_remote_copy(
                src_ref=part, dst_ref=part, send_sem=s_send.at[unit, k], recv_sem=s_recv.at[unit, k],
                device_id={"rep": sibling}, device_id_type=MESH,
            )
            for k, part in enumerate((slots.at[:, :, at], updates.at[:, at]))
        ]

    def out_copies(sems, unit, at):
        out = [pltpu.make_async_copy(updates.at[:, at], update_out.at[:, at], sems.at[unit, 4])]
        for d in range(4):
            from_shard = lax.rem(shard + 4 - d, 4)
            place = pl.ds(pl.multiple_of(from_shard * cols + at.start, GROUP), at.size)
            out.append(pltpu.make_async_copy(slots.at[d, :, at], weights_out.at[:, place], sems.at[unit, d]))
        return out

    def by_width(of_core, unit, act):
        @pl.when(unit < UNITS - 1)
        def _():
            act(span(of_core, unit))

        @pl.when(unit == UNITS - 1)
        def _():
            act(last_span(of_core))

    @pl.loop(0, UNITS)
    def _(unit):
        master_copy(unit).start()

    barrier = pltpu.get_barrier_semaphore()
    for peer in y_peers:
        pl.semaphore_signal(barrier, inc=1, device_id={"fsdp": peer}, device_id_type=MESH)
    for peer in x_peers + [sibling]:
        pl.semaphore_signal(barrier, inc=1, device_id={"rep": peer}, device_id_type=MESH)
    pl.semaphore_wait(barrier, 7)

    tables = shared_tables(table_ref)

    @pl.loop(0, UNITS + 3)
    def _(step):
        @pl.when(step < UNITS)
        def _():
            master_copy(step).wait()

            @pl.loop(0, 2)
            def _(k):
                g = first_group(core, step) + k
                lanes = pl.ds(pl.multiple_of(g * 64, 64), 64)
                at = pl.ds(pl.multiple_of(g * GROUP, GROUP), GROUP)
                update, weights = shared_group(band_ref[lanes, :], index_ref[lanes, :], masters[:, at], *tables)
                updates[:, at] = update
                slots[0, :, at] = weights

            for copy in y_copies(step):
                copy.start()

        @pl.when((step >= 1) & (step < UNITS + 1))
        def _():
            for copy in y_copies(step - 1):
                copy.wait_recv()
            for copy in x_copies(step - 1, False):
                copy.start()

        @pl.when((step >= 2) & (step < UNITS + 2))
        def _():
            unit = step - 2
            for copy in x_copies(unit, True):
                copy.wait_recv()

            def act(at):
                for copy in s_copies(unit, at):
                    copy.start()

            by_width(core, unit, act)
            for copy in out_copies(o_sem, unit, span(core, unit)):
                copy.start()

        @pl.when(step >= 3)
        def _():
            unit = step - 3

            def act(at):
                for copy in s_copies(unit, at):
                    copy.wait_recv()
                for copy in out_copies(t_sem, unit, at):
                    copy.start()

            by_width(1 - core, unit, act)

    @pl.loop(0, UNITS)
    def _(unit):
        for copy in y_copies(unit) + x_copies(unit, False):
            copy.wait_send()
        for copy in out_copies(o_sem, unit, span(core, unit)):
            copy.wait()

        def drain_own(at):
            for copy in s_copies(unit, at):
                copy.wait_send()

        def drain_other(at):
            for copy in out_copies(t_sem, unit, at):
                copy.wait()

        by_width(core, unit, drain_own)
        by_width(1 - core, unit, drain_other)


def update_part(bands, index, master):
    rows, cols = master.shape
    dma = pltpu.SemaphoreType.DMA
    table = shared_table_array()
    vmem = pl.BlockSpec(memory_space=pltpu.VMEM)
    anywhere = pl.BlockSpec(memory_space=pl.ANY)
    return pl.pallas_call(
        update_kernel,
        in_specs=[vmem, vmem, anywhere, vmem],
        out_specs=[anywhere, anywhere],
        out_shape=[
            jax.ShapeDtypeStruct(master.shape, f32),
            jax.ShapeDtypeStruct((rows, 4 * cols), bf16),
        ],
        scratch_shapes=[
            pltpu.VMEM((rows, cols), f32),
            pltpu.VMEM((rows, cols), f32),
            pltpu.VMEM((4, rows, cols), bf16),
            dma((UNITS,)), dma((UNITS, 3, 2)), dma((UNITS, 3, 2)), dma((UNITS, 3)), dma((UNITS, 3)),
            dma((UNITS, 2)), dma((UNITS, 2)), dma((UNITS, 5)), dma((UNITS, 5)),
        ],
        compiler_params=pltpu.CompilerParams(
            collective_id=1, has_side_effects=True, vmem_limit_bytes=VMEM_LIMIT
        ),
    )(bands, index, master, table)


def shards(grads, momentum, master, band_index):
    own = lax.axis_index("rep").astype(jnp.int32)[None]
    fresh, band = local_part(own, grads, momentum, band_index)
    bands, index = gather_part(band, band_index)
    update, weights_full = update_part(bands, index, master)
    return (fresh, update, weights_full)


def solution(mesh):
    in_specs = (
        P("rep", None, "fsdp"),
        P("rep", None, "fsdp"),
        P(None, "fsdp"),
        P(None, None, "fsdp"),
    )
    out_specs = (P("rep", None, "fsdp"), P(None, "fsdp"), P())
    return jax.shard_map(shards, mesh=mesh, in_specs=in_specs, out_specs=out_specs, check_vma=False)
```

```python
import jax
import jax.numpy as jnp
import numpy as np
import ml_dtypes
from jax import lax
from jax.experimental import pallas as pl
from jax.experimental.pallas import tpu as pltpu
from jax.sharding import PartitionSpec as P

BLOCK = 64
BAND = 16
GROUP = 256
PER_STEP = 3

momentum_decay = 0.9
learn_rate = 0.05

bf16 = jnp.bfloat16
f32 = jnp.float32
MESH = pl.DeviceIdType.MESH
VMEM_LIMIT = 60 * 2**20


def dct64():
    k = np.arange(BLOCK, dtype=np.float64)[:, None]
    n = np.arange(BLOCK, dtype=np.float64)[None, :]
    basis = np.cos(np.pi * (2.0 * n + 1.0) * k / (2.0 * BLOCK))
    return basis * np.where(k == 0.0, np.sqrt(1.0 / BLOCK), np.sqrt(2.0 / BLOCK))


def halves(table):
    hi = table.astype(np.float32).astype(ml_dtypes.bfloat16)
    lo = (table - hi.astype(np.float64)).astype(np.float32).astype(ml_dtypes.bfloat16)
    return hi, lo


def left_pair(table):
    hi, lo = halves(table)
    return np.concatenate([hi, hi], axis=1), lo


def make_tables():
    c = dct64()
    right = np.kron(np.eye(4), c.T)
    left = np.kron(np.eye(2), c)
    m, i = np.divmod(np.arange(BLOCK), 8)
    k1 = 4 * (m + 8 * (i // 4)) + i % 4
    back_perm = np.kron(np.eye(2), c[k1].T)
    spread = np.kron(np.eye(4), np.ones((BAND, BLOCK)))
    ones = np.kron(np.eye(4), np.ones((BLOCK, BLOCK)))
    as_bf16 = lambda a: a.astype(ml_dtypes.bfloat16)
    return dict(
        right=halves(right),
        right_t=halves(right.T),
        left=left_pair(left),
        left_t=left_pair(left.T),
        back=left_pair(back_perm),
        spread=as_bf16(spread),
        ones=as_bf16(ones),
    )


TABLES = make_tables()


def split(x):
    hi = x.astype(bf16)
    return hi, (x - hi.astype(f32)).astype(bf16)


def dot(a, b):
    return jnp.dot(a, b, preferred_element_type=f32)


def dot_nt(a, b):
    return lax.dot_general(a, b, (((1,), (1,)), ((), ())), preferred_element_type=f32)


def times_right(x, hi_ref, lo_ref):
    hi, lo = split(x)
    return dot(hi, hi_ref[...]) + (dot(lo, hi_ref[...]) + dot(hi, lo_ref[...]))


def times_left(pair_ref, lo_ref, x):
    hi, lo = split(x)
    return dot(pair_ref[...], jnp.concatenate([hi, lo], axis=0)) + dot(lo_ref[...], hi)


def summed_coefficients(band, index):
    reps = band.shape[1] // 2
    half = jnp.where(lax.broadcasted_iota(jnp.int32, (8, 2 * reps), 1) >= reps, 4, 0)
    eight = lax.broadcasted_iota(jnp.int32, (8, 2 * reps), 0)
    k2_of = lax.broadcasted_iota(jnp.int32, (BLOCK, 2 * reps), 0)
    zero = jnp.zeros((8, 2 * reps), f32)
    quarter = lax.broadcasted_iota(jnp.int32, (16, GROUP), 1) >> 6
    parts = []
    for p in range(2):
        values, codes, places = [], [], []
        for q in range(4):
            base = (p * 4 + q) * 8
            w = index[base : base + 8]
            values.append(band[base : base + 8])
            codes.append((w >> 6) + half)
            places.append(w & 63)
        for t in range(4):
            his, los, hots = [], [], []
            for q in range(4):
                a, b = [], []
                for m in (2 * t, 2 * t + 1):
                    spread = lambda x: jnp.broadcast_to(x[m : m + 1], eight.shape)
                    a.append(jnp.where(spread(codes[q]) == eight, spread(values[q]), 0.0))
                    here = jnp.broadcast_to(places[q][m : m + 1], k2_of.shape) == k2_of
                    b.append(jnp.where(here, 1.0, 0.0).astype(bf16))
                left = jnp.concatenate(
                    [jnp.concatenate([a[0], zero], axis=1), jnp.concatenate([zero, a[1]], axis=1)], axis=0
                )
                hi, lo = split(left)
                his.append(hi)
                los.append(lo)
                hots.append(jnp.concatenate(b, axis=1))
            out = dot_nt(jnp.concatenate(his + los, axis=0), jnp.concatenate(hots, axis=0))
            out = out[:64] + out[64:]
            rows = jnp.where(quarter == 0, out[:16], 0.0)
            for q in range(1, 4):
                rows = jnp.where(quarter == q, out[16 * q : 16 * (q + 1)], rows)
            parts.append(rows)
    return jnp.concatenate(parts, axis=0)


def shared_group(band, index, master, rt_hi, rt_lo, b_pair, b_lo, ones_ref):
    total = summed_coefficients(band, index)
    direction = times_left(b_pair, b_lo, times_right(total, rt_hi, rt_lo))
    square = direction * direction
    sums = [
        jnp.broadcast_to(jnp.sum(square[p * BLOCK : (p + 1) * BLOCK], axis=0, keepdims=True), (8, GROUP))
        for p in range(2)
    ]
    hi, lo = split(jnp.concatenate(sums, axis=0))
    means = (dot(hi, ones_ref[...]) + dot(lo, ones_ref[...])) * (1.0 / (BLOCK * BLOCK))
    scale = 0.1 * jnp.sqrt(means + 1e-06)
    scale = jnp.concatenate(
        [jnp.broadcast_to(scale[8 * p : 8 * p + 1], (BLOCK, GROUP)) for p in range(2)], axis=0
    )
    update = direction / (jnp.abs(direction) + scale)
    return update, (master - learn_rate * update).astype(bf16)


def rep_parts(r):
    return r // 16, (r // 2) % 8, r % 2


def rep_of(x, z, core):
    return x * 16 + z * 2 + core


UNITS = 7
WIDE = 2 * GROUP
STEPS = 9
EARLY, MIDDLE = 2, 6


def kernel(
    grads_ref, mom_ref, index_ref, master_ref, table_ref,
    fresh_out, update_out, weights_out,
    grads, acc, kept_rows, wide, own_index, index_rows, places, rows, masters, updates, slots, table,
    in_sem, index_sem, f_sem, gz_send, gz_recv, gx_send, gx_recv, gs_send, gs_recv,
    m_sem, y_send, y_recv, x_send, x_recv, z_send, z_recv, s_send, s_recv, o_sem, t_sem,
):
    rep = lax.axis_index("rep")
    shard = lax.axis_index("fsdp")
    x, z, core = rep_parts(rep)
    cols = masters.shape[1]
    groups = cols // GROUP
    sibling = rep_of(x, z, 1 - core)
    y_peers = [lax.rem(shard + d, 4) for d in range(1, 4)]
    x_peers = [rep_of(lax.rem(x + d, 4), z, core) for d in range(1, 4)]
    z_peers = [rep_of(x, lax.rem(z + d, 8), core) for d in range(1, 8)]
    chunk = PER_STEP * GROUP
    tall = PER_STEP * 2 * BLOCK

    def remote(src, dst, send, recv, peer):
        return pltpu.make_async_remote_copy(
            src_ref=src, dst_ref=dst, send_sem=send, recv_sem=recv, device_id=peer, device_id_type=MESH,
        )


    def columns(step):
        return pl.ds(pl.multiple_of(step * chunk, chunk), chunk)

    def in_copies(step):
        at = columns(step)
        return (
            pltpu.make_async_copy(grads_ref.at[0, :, at], grads.at[:, at], in_sem.at[step, 0]),
            pltpu.make_async_copy(mom_ref.at[0, :, at], acc.at[:, at], in_sem.at[step, 1]),
        )

    def fresh_copy(step):
        at = columns(step)
        return pltpu.make_async_copy(acc.at[:, at], fresh_out.at[0, :, at], f_sem.at[step])

    def first_group(of_core, unit):
        return 2 * unit + of_core * (groups - 2 - 4 * unit)

    def span(of_core, unit):
        return pl.ds(pl.multiple_of(first_group(of_core, unit) * GROUP, GROUP), WIDE)

    def last_span(of_core):
        return pl.ds(pl.multiple_of((groups // 2 - 1 + 2 * of_core) * GROUP, GROUP), GROUP)

    def master_copy(unit):
        at = span(core, unit)
        return pltpu.make_async_copy(master_ref.at[:, at], masters.at[:, at], m_sem.at[unit])

    pull_own = pltpu.make_async_copy(index_ref.at[x, z, core], own_index, index_sem.at[2])
    pull_table = pltpu.make_async_copy(table_ref, table, index_sem.at[3])
    pulls = [pltpu.make_async_copy(index_ref.at[:, :, c], index_rows.at[c], index_sem.at[c]) for c in range(2)]
    pull_own.start()
    pull_table.start()

    @pl.loop(0, STEPS)
    def _(step):
        for copy in in_copies(step):
            copy.start()

    for pull in pulls:
        pull.start()

    @pl.loop(0, UNITS)
    def _(unit):
        master_copy(unit).start()

    barrier = pltpu.get_barrier_semaphore()
    for peer in y_peers:
        pl.semaphore_signal(barrier, inc=1, device_id={"fsdp": peer}, device_id_type=MESH)
    for peer in x_peers + z_peers + [sibling]:
        pl.semaphore_signal(barrier, inc=1, device_id={"rep": peer}, device_id_type=MESH)


    r_hi, r_lo, rt_hi, rt_lo, ones = (table.at[k * 256 : (k + 1) * 256] for k in range(5))
    l_pair, lt_pair, b_pair = (table.at[1280 + k * 128 : 1408 + k * 128] for k in range(3))
    l_lo, lt_lo = (table.at[1664:1792, k * 128 : (k + 1) * 128] for k in range(2))
    b_lo = table.at[1792:1920, 0:128]
    spread_ref = table.at[1920:1984]

    pull_own.wait()
    row = lax.broadcasted_iota(jnp.int32, (BLOCK, groups * BLOCK), 0)
    lane = lax.broadcasted_iota(jnp.int32, (BLOCK, groups * BLOCK), 1)
    own_slot = (lane & (BAND - 1)) == (row >> 2)
    for p in range(2):
        within = own_index[p : p + 1, :] & 255
        placed = jnp.where(own_slot, jnp.broadcast_to(within, own_slot.shape), 0).astype(f32)
        for g in range(groups):
            at = (2 * g + p) * BLOCK
            wide[at : at + BLOCK, :] = placed[:, g * BLOCK : (g + 1) * BLOCK].astype(bf16)
    pull_table.wait()

    mine = core * 32 + x * 8 + z

    @pl.loop(0, STEPS)
    def _(step):
        for copy in in_copies(step):
            copy.wait()
        at = columns(step)
        total = momentum_decay * acc[:, at] + grads[:, at].astype(f32)
        acc[:, at] = total
        stacked = jnp.concatenate([total[:, g * GROUP : (g + 1) * GROUP] for g in range(PER_STEP)], axis=0)
        half = times_right(stacked, r_hi, r_lo)
        coeff = jnp.concatenate(
            [times_left(l_pair, l_lo, half[g * 128 : (g + 1) * 128]) for g in range(PER_STEP)], axis=0
        )
        tall_at = pl.ds(pl.multiple_of(step * tall, tall), tall)
        index = dot(wide[tall_at, :], spread_ref[...])
        row = lax.broadcasted_iota(jnp.int32, (tall, GROUP), 0)
        lane = lax.broadcasted_iota(jnp.int32, (tall, GROUP), 1)
        place = (((row & 3) << 6) + (lane & 63)).astype(f32)
        kept = jnp.where(index == place, coeff, 0.0)
        kept_rows[tall_at, :] = kept
        hi, mid = split(kept)
        low = (kept - hi.astype(f32) - mid.astype(f32)).astype(bf16)
        sums = dot_nt(hi, spread_ref[...]) + (dot_nt(mid, spread_ref[...]) + dot_nt(low, spread_ref[...]))
        zrow = lax.broadcasted_iota(jnp.int32, (tall, BLOCK), 0)
        zlane = lax.broadcasted_iota(jnp.int32, (tall, BLOCK), 1)
        sums = jnp.where((zlane & (BAND - 1)) == ((zrow & 63) >> 2), sums, 0.0)
        for g in range(PER_STEP):
            pair = [
                jnp.sum(sums[(2 * g + p) * BLOCK : (2 * g + p + 1) * BLOCK], axis=0, keepdims=True)
                for p in range(2)
            ]
            rows[mine, pl.ds(step * PER_STEP + g, 1), :] = jnp.concatenate(pair, axis=1)

    def inverse_turn(step):
        half = times_right(kept_rows[pl.ds(pl.multiple_of(step * tall, tall), tall), :], rt_hi, rt_lo)
        for g in range(PER_STEP):
            at = pl.ds(pl.multiple_of(step * chunk + g * GROUP, GROUP), GROUP)
            acc[:, at] = acc[:, at] - times_left(lt_pair, lt_lo, half[g * 128 : (g + 1) * 128])
        fresh_copy(step).start()


    pl.semaphore_wait(barrier, 14)
    own = rows.at[mine]
    gz = [remote(own, own, gz_send.at[d], gz_recv.at[d], {"rep": peer}) for d, peer in enumerate(z_peers)]
    for copy in gz:
        copy.start()

    for pull in pulls:
        pull.wait()
    for p in range(2):
        for k in range((groups + 1) // 2):
            lanes = min(128, groups * BLOCK - k * 128)
            part = index_rows[:, :, :, p, k * 128 : k * 128 + lanes].reshape(64, lanes)
            turned = part.T & 255
            for b in range(lanes // BAND):
                at = (((2 * k + b // 4) * 2 + p) * 4 + b % 4) * 8
                places[at : at + 8, :] = jnp.concatenate(
                    [turned[b * 16 : b * 16 + 8], turned[b * 16 + 8 : b * 16 + 16]], axis=1
                )
    pl.loop(0, EARLY)(inverse_turn)

    for copy in gz:
        copy.wait()

    def bundle(of_x):
        return rows.at[pl.ds(core * 32 + of_x * 8, 8)]

    gx = [remote(bundle(x), bundle(x), gx_send.at[d], gx_recv.at[d], {"rep": peer}) for d, peer in enumerate(x_peers)]
    for copy in gx:
        copy.start()
    gs = [remote(bundle(x), bundle(x), gs_send.at[0], gs_recv.at[0], {"rep": sibling})]
    gs[0].start()
    pl.loop(EARLY, MIDDLE)(inverse_turn)
    for d in range(1, 4):
        gx[d - 1].wait_recv()
        part = bundle(lax.rem(x + 4 - d, 4))
        copy = remote(part, part, gs_send.at[d], gs_recv.at[d], {"rep": sibling})
        copy.start()
        gs.append(copy)
    for copy in gx:
        copy.wait_send()
    for copy in gs:
        copy.wait()


    def y_copies(unit):
        at = span(core, unit)
        parts = (
            (pl.ds(0, 32), at),
            (x_rows(x), at),
            z_part(z, unit),
        )
        return [
            remote(
                slots.at[0, rows_at, cols_at], slots.at[d + 1, rows_at, cols_at],
                y_send.at[unit, d, k], y_recv.at[unit, d, k], {"fsdp": y_peers[d]},
            )
            for d in range(3)
            for k, (rows_at, cols_at) in enumerate(parts)
        ]

    def x_rows(of_x):
        return pl.ds(pl.multiple_of(32 + of_x * 16, 16), 16)

    def z_part(of_z, unit):
        start = first_group(core, unit) * GROUP + (of_z % 4) * 128
        return pl.ds(pl.multiple_of(96 + (of_z // 4) * 16, 16), 16), pl.ds(pl.multiple_of(start, 128), 128)

    def onward_copies(unit, arriving):
        at = span(core, unit)
        out = []
        for d in range(3):
            part = slots.at[pl.ds(1, 3), x_rows(lax.rem(x + 3 - d, 4) if arriving else x), at]
            out.append(remote(part, part, x_send.at[unit, d], x_recv.at[unit, d], {"rep": x_peers[d]}))
        for d in range(7):
            rows_at, cols_at = z_part(lax.rem(z + 7 - d, 8) if arriving else z, unit)
            part = slots.at[pl.ds(1, 3), rows_at, cols_at]
            out.append(remote(part, part, z_send.at[unit, d], z_recv.at[unit, d], {"rep": z_peers[d]}))
        return out

    def s_copies(unit, at):
        return [
            remote(part, part, s_send.at[unit, k], s_recv.at[unit, k], {"rep": sibling})
            for k, part in enumerate((slots.at[:, :, at], updates.at[:, at]))
        ]

    def out_copies(sems, unit, at):
        out = [pltpu.make_async_copy(updates.at[:, at], update_out.at[:, at], sems.at[unit, 4])]
        for d in range(4):
            from_shard = lax.rem(shard + 4 - d, 4)
            place = pl.ds(pl.multiple_of(from_shard * cols + at.start, GROUP), at.size)
            out.append(pltpu.make_async_copy(slots.at[d, :, at], weights_out.at[:, place], sems.at[unit, d]))
        return out

    def by_width(of_core, unit, act):
        @pl.when(unit < UNITS - 1)
        def _():
            act(span(of_core, unit))

        @pl.when(unit == UNITS - 1)
        def _():
            act(last_span(of_core))

    tables = (rt_hi, rt_lo, b_pair, b_lo, ones)

    @pl.loop(0, UNITS + 3)
    def _(step):
        @pl.when(step < UNITS)
        def _():
            master_copy(step).wait()
            for k in range(2):
                g = first_group(core, step) + k
                turned = rows[:, g, :].T
                band = jnp.concatenate(
                    [
                        jnp.concatenate([turned[b * 16 : b * 16 + 8], turned[b * 16 + 8 : b * 16 + 16]], axis=1)
                        for b in range(8)
                    ],
                    axis=0,
                )
                lanes = pl.ds(pl.multiple_of(g * 64, 64), 64)
                at = pl.ds(pl.multiple_of(g * GROUP, GROUP), GROUP)
                update, weights = shared_group(band, places[lanes, :], masters[:, at], *tables)
                updates[:, at] = update
                slots[0, :, at] = weights
            for copy in y_copies(step):
                copy.start()

        @pl.when((step >= 1) & (step < UNITS + 1))
        def _():
            for copy in y_copies(step - 1):
                copy.wait_recv()
            for copy in onward_copies(step - 1, False):
                copy.start()

        @pl.when(step >= UNITS)
        def _():
            inverse_turn(MIDDLE + step - UNITS)

        @pl.when((step >= 2) & (step < UNITS + 2))
        def _():
            unit = step - 2
            for copy in onward_copies(unit, True):
                copy.wait_recv()

            def act(at):
                for copy in s_copies(unit, at):
                    copy.start()

            by_width(core, unit, act)
            for copy in out_copies(o_sem, unit, span(core, unit)):
                copy.start()

        @pl.when(step >= 3)
        def _():
            unit = step - 3

            def act(at):
                for copy in s_copies(unit, at):
                    copy.wait_recv()
                for copy in out_copies(t_sem, unit, at):
                    copy.start()

            by_width(1 - core, unit, act)

    @pl.loop(0, STEPS)
    def _(step):
        fresh_copy(step).wait()

    @pl.loop(0, UNITS)
    def _(unit):
        for copy in y_copies(unit) + onward_copies(unit, False):
            copy.wait_send()
        for copy in out_copies(o_sem, unit, span(core, unit)):
            copy.wait()

        def drain_own(at):
            for copy in s_copies(unit, at):
                copy.wait_send()

        def drain_other(at):
            for copy in out_copies(t_sem, unit, at):
                copy.wait()

        by_width(core, unit, drain_own)
        by_width(1 - core, unit, drain_other)


def table_array():
    t = TABLES
    beside = lambda a, b: np.concatenate([a, b], axis=1)
    parts = [
        *t["right"], *t["right_t"], t["ones"], t["left"][0], t["left_t"][0], t["back"][0],
        beside(t["left"][1], t["left_t"][1]), beside(t["back"][1], t["back"][1]), t["spread"],
    ]
    return jnp.asarray(np.concatenate(parts, axis=0))


def shards(grads, momentum, master, band_index):
    rows, cols = master.shape
    reps, _, lanes = band_index.shape
    groups = cols // GROUP
    dma = pltpu.SemaphoreType.DMA
    table = table_array()
    anywhere = pl.BlockSpec(memory_space=pl.ANY)
    vmem = pltpu.VMEM
    return tuple(pl.pallas_call(
        kernel,
        in_specs=[anywhere] * 5,
        out_specs=[anywhere] * 3,
        out_shape=[
            jax.ShapeDtypeStruct(momentum.shape, f32),
            jax.ShapeDtypeStruct(master.shape, f32),
            jax.ShapeDtypeStruct((rows, 4 * cols), bf16),
        ],
        scratch_shapes=[
            vmem((rows, cols), bf16),
            vmem((rows, cols), f32),
            vmem((groups * rows, GROUP), f32),
            vmem((groups * rows, BLOCK), bf16),
            vmem((2, lanes), jnp.int32),
            vmem((2, 4, 8, 2, lanes), jnp.int32),
            vmem((groups * 64, 128), jnp.int32),
            vmem((reps, groups, 128), f32),
            vmem((rows, cols), f32),
            vmem((rows, cols), f32),
            vmem((4, rows, cols), bf16),
            vmem(table.shape, bf16),
            dma((STEPS, 2)), dma((4,)), dma((STEPS,)),
            dma((7,)), dma((7,)), dma((3,)), dma((3,)), dma((4,)), dma((4,)),
            dma((UNITS,)), dma((UNITS, 3, 3)), dma((UNITS, 3, 3)), dma((UNITS, 3)), dma((UNITS, 3)),
            dma((UNITS, 7)), dma((UNITS, 7)), dma((UNITS, 2)), dma((UNITS, 2)), dma((UNITS, 5)), dma((UNITS, 5)),
        ],
        compiler_params=pltpu.CompilerParams(
            collective_id=0, has_side_effects=True, vmem_limit_bytes=VMEM_LIMIT
        ),
    )(grads, momentum, band_index.reshape(4, 8, 2, 2, lanes), master, table))


def solution(mesh):
    in_specs = (
        P("rep", None, "fsdp"),
        P("rep", None, "fsdp"),
        P(None, "fsdp"),
        P(None, None, "fsdp"),
    )
    out_specs = (P("rep", None, "fsdp"), P(None, "fsdp"), P())
    return jax.shard_map(shards, mesh=mesh, in_specs=in_specs, out_specs=out_specs, check_vma=False)
```

```python
import jax
import jax.numpy as jnp
import numpy as np
import ml_dtypes
from jax import lax
from jax.experimental import pallas as pl
from jax.experimental.pallas import tpu as pltpu
from jax.sharding import PartitionSpec as P

BLOCK = 64
BAND = 16
GROUP = 256
PER_STEP = 3

momentum_decay = 0.9
learn_rate = 0.05

bf16 = jnp.bfloat16
f32 = jnp.float32
MESH = pl.DeviceIdType.MESH
VMEM_LIMIT = 60 * 2**20


def dct64():
    k = np.arange(BLOCK, dtype=np.float64)[:, None]
    n = np.arange(BLOCK, dtype=np.float64)[None, :]
    basis = np.cos(np.pi * (2.0 * n + 1.0) * k / (2.0 * BLOCK))
    return basis * np.where(k == 0.0, np.sqrt(1.0 / BLOCK), np.sqrt(2.0 / BLOCK))


def halves(table):
    hi = table.astype(np.float32).astype(ml_dtypes.bfloat16)
    lo = (table - hi.astype(np.float64)).astype(np.float32).astype(ml_dtypes.bfloat16)
    return hi, lo


def left_pair(table):
    hi, lo = halves(table)
    return np.concatenate([hi, hi], axis=1), lo


def make_tables():
    c = dct64()
    right = np.kron(np.eye(4), c.T)
    left = np.kron(np.eye(2), c)
    m, i = np.divmod(np.arange(BLOCK), 8)
    k1 = 4 * (m + 8 * (i // 4)) + i % 4
    back_perm = np.kron(np.eye(2), c[k1].T)
    spread = np.kron(np.eye(4), np.ones((BAND, BLOCK)))
    ones = np.kron(np.eye(4), np.ones((BLOCK, BLOCK)))
    as_bf16 = lambda a: a.astype(ml_dtypes.bfloat16)
    return dict(
        right=halves(right),
        right_t=halves(right.T),
        left=left_pair(left),
        left_t=left_pair(left.T),
        back=left_pair(back_perm),
        spread=as_bf16(spread),
        ones=as_bf16(ones),
    )


TABLES = make_tables()


def split(x):
    hi = x.astype(bf16)
    return hi, (x - hi.astype(f32)).astype(bf16)


def dot(a, b):
    return jnp.dot(a, b, preferred_element_type=f32)


def dot_nt(a, b):
    return lax.dot_general(a, b, (((1,), (1,)), ((), ())), preferred_element_type=f32)


def times_right(x, hi_ref, lo_ref):
    hi, lo = split(x)
    return dot(hi, hi_ref[...]) + (dot(lo, hi_ref[...]) + dot(hi, lo_ref[...]))


def times_left(pair_ref, lo_ref, x):
    hi, lo = split(x)
    return dot(pair_ref[...], jnp.concatenate([hi, lo], axis=0)) + dot(lo_ref[...], hi)


def summed_coefficients(band, index):
    reps = band.shape[1] // 2
    half = jnp.where(lax.broadcasted_iota(jnp.int32, (8, 2 * reps), 1) >= reps, 4, 0)
    eight = lax.broadcasted_iota(jnp.int32, (8, 2 * reps), 0)
    k2_of = lax.broadcasted_iota(jnp.int32, (BLOCK, 2 * reps), 0)
    zero = jnp.zeros((8, 2 * reps), f32)
    quarter = lax.broadcasted_iota(jnp.int32, (16, GROUP), 1) >> 6
    parts = []
    for p in range(2):
        values, codes, places = [], [], []
        for q in range(4):
            base = (p * 4 + q) * 8
            w = index[base : base + 8]
            values.append(band[base : base + 8])
            codes.append((w >> 6) + half)
            places.append(w & 63)
        for t in range(4):
            his, los, hots = [], [], []
            for q in range(4):
                a, b = [], []
                for m in (2 * t, 2 * t + 1):
                    spread = lambda x: jnp.broadcast_to(x[m : m + 1], eight.shape)
                    a.append(jnp.where(spread(codes[q]) == eight, spread(values[q]), 0.0))
                    here = jnp.broadcast_to(places[q][m : m + 1], k2_of.shape) == k2_of
                    b.append(jnp.where(here, 1.0, 0.0).astype(bf16))
                left = jnp.concatenate(
                    [jnp.concatenate([a[0], zero], axis=1), jnp.concatenate([zero, a[1]], axis=1)], axis=0
                )
                hi, lo = split(left)
                his.append(hi)
                los.append(lo)
                hots.append(jnp.concatenate(b, axis=1))
            out = dot_nt(jnp.concatenate(his + los, axis=0), jnp.concatenate(hots, axis=0))
            out = out[:64] + out[64:]
            rows = jnp.where(quarter == 0, out[:16], 0.0)
            for q in range(1, 4):
                rows = jnp.where(quarter == q, out[16 * q : 16 * (q + 1)], rows)
            parts.append(rows)
    return jnp.concatenate(parts, axis=0)


def shared_group(band, index, master, rt_hi, rt_lo, b_pair, b_lo, ones_ref):
    total = summed_coefficients(band, index)
    direction = times_left(b_pair, b_lo, times_right(total, rt_hi, rt_lo))
    square = direction * direction
    sums = [
        jnp.broadcast_to(jnp.sum(square[p * BLOCK : (p + 1) * BLOCK], axis=0, keepdims=True), (8, GROUP))
        for p in range(2)
    ]
    hi, lo = split(jnp.concatenate(sums, axis=0))
    means = (dot(hi, ones_ref[...]) + dot(lo, ones_ref[...])) * (1.0 / (BLOCK * BLOCK))
    scale = 0.1 * jnp.sqrt(means + 1e-06)
    scale = jnp.concatenate(
        [jnp.broadcast_to(scale[8 * p : 8 * p + 1], (BLOCK, GROUP)) for p in range(2)], axis=0
    )
    update = direction / (jnp.abs(direction) + scale)
    return update, (master - learn_rate * update).astype(bf16)


def rep_parts(r):
    return r // 16, (r // 2) % 8, r % 2


def rep_of(x, z, core):
    return x * 16 + z * 2 + core


UNITS = 7
WIDE = 2 * GROUP
Y_AFTER, ONWARD_AFTER, SWAP_AFTER = 2, 4, 6
STEPS = 9
EARLY, MIDDLE = 2, 6


def kernel(
    grads_ref, mom_ref, index_ref, master_ref, table_ref,
    fresh_out, update_out, weights_out,
    grads, acc, kept_rows, wide, own_index, index_rows, places, rows, masters, updates, slots, table,
    in_sem, index_sem, f_sem, gz_send, gz_recv, gx_send, gx_recv, gs_send, gs_recv,
    m_sem, y_send, y_recv, x_send, x_recv, z_send, z_recv, s_send, s_recv, o_sem, t_sem,
):
    rep = lax.axis_index("rep")
    shard = lax.axis_index("fsdp")
    x, z, core = rep_parts(rep)
    cols = masters.shape[1]
    groups = cols // GROUP
    sibling = rep_of(x, z, 1 - core)
    y_peers = [lax.rem(shard + d, 4) for d in range(1, 4)]
    x_peers = [rep_of(lax.rem(x + d, 4), z, core) for d in range(1, 4)]
    z_peers = [rep_of(x, lax.rem(z + d, 8), core) for d in range(1, 8)]
    chunk = PER_STEP * GROUP
    tall = PER_STEP * 2 * BLOCK

    def remote(src, dst, send, recv, peer):
        return pltpu.make_async_remote_copy(
            src_ref=src, dst_ref=dst, send_sem=send, recv_sem=recv, device_id=peer, device_id_type=MESH,
        )


    def columns(step):
        return pl.ds(pl.multiple_of(step * chunk, chunk), chunk)

    def in_copies(step):
        at = columns(step)
        return (
            pltpu.make_async_copy(grads_ref.at[0, :, at], grads.at[:, at], in_sem.at[step, 0]),
            pltpu.make_async_copy(mom_ref.at[0, :, at], acc.at[:, at], in_sem.at[step, 1]),
        )

    def fresh_copy(step):
        at = columns(step)
        return pltpu.make_async_copy(acc.at[:, at], fresh_out.at[0, :, at], f_sem.at[step])

    def first_group(of_core, unit):
        return 2 * unit + of_core * (groups - 2 - 4 * unit)

    def span(of_core, unit):
        return pl.ds(pl.multiple_of(first_group(of_core, unit) * GROUP, GROUP), WIDE)

    def last_span(of_core):
        return pl.ds(pl.multiple_of((groups // 2 - 1 + 2 * of_core) * GROUP, GROUP), GROUP)

    def master_copy(unit):
        at = span(core, unit)
        return pltpu.make_async_copy(master_ref.at[:, at], masters.at[:, at], m_sem.at[unit])

    pull_own = pltpu.make_async_copy(index_ref.at[x, z, core], own_index, index_sem.at[2])
    pull_table = pltpu.make_async_copy(table_ref, table, index_sem.at[3])
    pulls = [pltpu.make_async_copy(index_ref.at[:, :, c], index_rows.at[c], index_sem.at[c]) for c in range(2)]
    pull_own.start()
    pull_table.start()

    @pl.loop(0, STEPS)
    def _(step):
        for copy in in_copies(step):
            copy.start()

    for pull in pulls:
        pull.start()

    @pl.loop(0, UNITS)
    def _(unit):
        master_copy(unit).start()

    barrier = pltpu.get_barrier_semaphore()
    for peer in y_peers:
        pl.semaphore_signal(barrier, inc=1, device_id={"fsdp": peer}, device_id_type=MESH)
    for peer in x_peers + z_peers + [sibling]:
        pl.semaphore_signal(barrier, inc=1, device_id={"rep": peer}, device_id_type=MESH)


    r_hi, r_lo, rt_hi, rt_lo, ones = (table.at[k * 256 : (k + 1) * 256] for k in range(5))
    l_pair, lt_pair, b_pair = (table.at[1280 + k * 128 : 1408 + k * 128] for k in range(3))
    l_lo, lt_lo = (table.at[1664:1792, k * 128 : (k + 1) * 128] for k in range(2))
    b_lo = table.at[1792:1920, 0:128]
    spread_ref = table.at[1920:1984]

    pull_own.wait()
    row = lax.broadcasted_iota(jnp.int32, (BLOCK, groups * BLOCK), 0)
    lane = lax.broadcasted_iota(jnp.int32, (BLOCK, groups * BLOCK), 1)
    own_slot = (lane & (BAND - 1)) == (row >> 2)
    for p in range(2):
        within = own_index[p : p + 1, :] & 255
        placed = jnp.where(own_slot, jnp.broadcast_to(within, own_slot.shape), 0).astype(f32)
        for g in range(groups):
            at = (2 * g + p) * BLOCK
            wide[at : at + BLOCK, :] = placed[:, g * BLOCK : (g + 1) * BLOCK].astype(bf16)
    pull_table.wait()

    mine = core * 32 + x * 8 + z

    @pl.loop(0, STEPS)
    def _(step):
        for copy in in_copies(step):
            copy.wait()
        at = columns(step)
        total = momentum_decay * acc[:, at] + grads[:, at].astype(f32)
        acc[:, at] = total
        stacked = jnp.concatenate([total[:, g * GROUP : (g + 1) * GROUP] for g in range(PER_STEP)], axis=0)
        half = times_right(stacked, r_hi, r_lo)
        coeff = jnp.concatenate(
            [times_left(l_pair, l_lo, half[g * 128 : (g + 1) * 128]) for g in range(PER_STEP)], axis=0
        )
        tall_at = pl.ds(pl.multiple_of(step * tall, tall), tall)
        index = dot(wide[tall_at, :], spread_ref[...])
        row = lax.broadcasted_iota(jnp.int32, (tall, GROUP), 0)
        lane = lax.broadcasted_iota(jnp.int32, (tall, GROUP), 1)
        place = (((row & 3) << 6) + (lane & 63)).astype(f32)
        kept = jnp.where(index == place, coeff, 0.0)
        kept_rows[tall_at, :] = kept
        hi, mid = split(kept)
        low = (kept - hi.astype(f32) - mid.astype(f32)).astype(bf16)
        sums = dot_nt(hi, spread_ref[...]) + (dot_nt(mid, spread_ref[...]) + dot_nt(low, spread_ref[...]))
        zrow = lax.broadcasted_iota(jnp.int32, (tall, BLOCK), 0)
        zlane = lax.broadcasted_iota(jnp.int32, (tall, BLOCK), 1)
        sums = jnp.where((zlane & (BAND - 1)) == ((zrow & 63) >> 2), sums, 0.0)
        for g in range(PER_STEP):
            pair = [
                jnp.sum(sums[(2 * g + p) * BLOCK : (2 * g + p + 1) * BLOCK], axis=0, keepdims=True)
                for p in range(2)
            ]
            rows[mine, pl.ds(step * PER_STEP + g, 1), :] = jnp.concatenate(pair, axis=1)

    def inverse_turn(step):
        half = times_right(kept_rows[pl.ds(pl.multiple_of(step * tall, tall), tall), :], rt_hi, rt_lo)
        for g in range(PER_STEP):
            at = pl.ds(pl.multiple_of(step * chunk + g * GROUP, GROUP), GROUP)
            acc[:, at] = acc[:, at] - times_left(lt_pair, lt_lo, half[g * 128 : (g + 1) * 128])
        fresh_copy(step).start()


    pl.semaphore_wait(barrier, 14)
    own = rows.at[mine]
    gz = [remote(own, own, gz_send.at[d], gz_recv.at[d], {"rep": peer}) for d, peer in enumerate(z_peers)]
    for copy in gz:
        copy.start()

    for pull in pulls:
        pull.wait()
    for p in range(2):
        for k in range((groups + 1) // 2):
            lanes = min(128, groups * BLOCK - k * 128)
            part = index_rows[:, :, :, p, k * 128 : k * 128 + lanes].reshape(64, lanes)
            turned = part.T & 255
            for b in range(lanes // BAND):
                at = (((2 * k + b // 4) * 2 + p) * 4 + b % 4) * 8
                places[at : at + 8, :] = jnp.concatenate(
                    [turned[b * 16 : b * 16 + 8], turned[b * 16 + 8 : b * 16 + 16]], axis=1
                )
    pl.loop(0, EARLY)(inverse_turn)

    for copy in gz:
        copy.wait()

    def bundle(of_x):
        return rows.at[pl.ds(core * 32 + of_x * 8, 8)]

    gx = [remote(bundle(x), bundle(x), gx_send.at[d], gx_recv.at[d], {"rep": peer}) for d, peer in enumerate(x_peers)]
    for copy in gx:
        copy.start()
    gs = [remote(bundle(x), bundle(x), gs_send.at[0], gs_recv.at[0], {"rep": sibling})]
    gs[0].start()
    pl.loop(EARLY, MIDDLE)(inverse_turn)
    for d in range(1, 4):
        gx[d - 1].wait_recv()
        part = bundle(lax.rem(x + 4 - d, 4))
        copy = remote(part, part, gs_send.at[d], gs_recv.at[d], {"rep": sibling})
        copy.start()
        gs.append(copy)
    for copy in gx:
        copy.wait_send()
    for copy in gs:
        copy.wait()


    def y_copies(unit):
        at = span(core, unit)
        parts = (
            (pl.ds(0, 32), at),
            (x_rows(x), at),
            z_part(z, unit),
        )
        return [
            remote(
                slots.at[0, rows_at, cols_at], slots.at[d + 1, rows_at, cols_at],
                y_send.at[unit, d, k], y_recv.at[unit, d, k], {"fsdp": y_peers[d]},
            )
            for d in range(3)
            for k, (rows_at, cols_at) in enumerate(parts)
        ]

    def x_rows(of_x):
        return pl.ds(pl.multiple_of(32 + of_x * 16, 16), 16)

    def z_part(of_z, unit):
        start = first_group(core, unit) * GROUP + (of_z % 4) * 128
        return pl.ds(pl.multiple_of(96 + (of_z // 4) * 16, 16), 16), pl.ds(pl.multiple_of(start, 128), 128)

    def onward_copies(unit, arriving):
        at = span(core, unit)
        out = []
        for d in range(3):
            part = slots.at[pl.ds(1, 3), x_rows(lax.rem(x + 3 - d, 4) if arriving else x), at]
            out.append(remote(part, part, x_send.at[unit, d], x_recv.at[unit, d], {"rep": x_peers[d]}))
        for d in range(7):
            rows_at, cols_at = z_part(lax.rem(z + 7 - d, 8) if arriving else z, unit)
            part = slots.at[pl.ds(1, 3), rows_at, cols_at]
            out.append(remote(part, part, z_send.at[unit, d], z_recv.at[unit, d], {"rep": z_peers[d]}))
        return out

    def s_copies(unit, at):
        return [
            remote(part, part, s_send.at[unit, k], s_recv.at[unit, k], {"rep": sibling})
            for k, part in enumerate((slots.at[:, :, at], updates.at[:, at]))
        ]

    def out_copies(sems, unit, at):
        out = [pltpu.make_async_copy(updates.at[:, at], update_out.at[:, at], sems.at[unit, 4])]
        for d in range(4):
            from_shard = lax.rem(shard + 4 - d, 4)
            place = pl.ds(pl.multiple_of(from_shard * cols + at.start, GROUP), at.size)
            out.append(pltpu.make_async_copy(slots.at[d, :, at], weights_out.at[:, place], sems.at[unit, d]))
        return out

    def by_width(of_core, unit, act):
        @pl.when(unit < UNITS - 1)
        def _():
            act(span(of_core, unit))

        @pl.when(unit == UNITS - 1)
        def _():
            act(last_span(of_core))

    tables = (rt_hi, rt_lo, b_pair, b_lo, ones)

    @pl.loop(0, UNITS + SWAP_AFTER)
    def _(step):
        @pl.when(step < UNITS)
        def _():
            master_copy(step).wait()
            for k in range(2):
                g = first_group(core, step) + k
                turned = rows[:, g, :].T
                band = jnp.concatenate(
                    [
                        jnp.concatenate([turned[b * 16 : b * 16 + 8], turned[b * 16 + 8 : b * 16 + 16]], axis=1)
                        for b in range(8)
                    ],
                    axis=0,
                )
                lanes = pl.ds(pl.multiple_of(g * 64, 64), 64)
                at = pl.ds(pl.multiple_of(g * GROUP, GROUP), GROUP)
                update, weights = shared_group(band, places[lanes, :], masters[:, at], *tables)
                updates[:, at] = update
                slots[0, :, at] = weights
            for copy in y_copies(step):
                copy.start()

        @pl.when((step >= Y_AFTER) & (step < UNITS + Y_AFTER))
        def _():
            for copy in y_copies(step - Y_AFTER):
                copy.wait_recv()
            for copy in onward_copies(step - Y_AFTER, False):
                copy.start()

        @pl.when((step >= UNITS) & (step < UNITS + STEPS - MIDDLE))
        def _():
            inverse_turn(MIDDLE + step - UNITS)

        @pl.when((step >= ONWARD_AFTER) & (step < UNITS + ONWARD_AFTER))
        def _():
            unit = step - ONWARD_AFTER
            for copy in onward_copies(unit, True):
                copy.wait_recv()

            def act(at):
                for copy in s_copies(unit, at):
                    copy.start()

            by_width(core, unit, act)
            for copy in out_copies(o_sem, unit, span(core, unit)):
                copy.start()

        @pl.when(step >= SWAP_AFTER)
        def _():
            unit = step - SWAP_AFTER

            def act(at):
                for copy in s_copies(unit, at):
                    copy.wait_recv()
                for copy in out_copies(t_sem, unit, at):
                    copy.start()

            by_width(1 - core, unit, act)

    @pl.loop(0, STEPS)
    def _(step):
        fresh_copy(step).wait()

    @pl.loop(0, UNITS)
    def _(unit):
        for copy in y_copies(unit) + onward_copies(unit, False):
            copy.wait_send()
        for copy in out_copies(o_sem, unit, span(core, unit)):
            copy.wait()

        def drain_own(at):
            for copy in s_copies(unit, at):
                copy.wait_send()

        def drain_other(at):
            for copy in out_copies(t_sem, unit, at):
                copy.wait()

        by_width(core, unit, drain_own)
        by_width(1 - core, unit, drain_other)


def table_array():
    t = TABLES
    beside = lambda a, b: np.concatenate([a, b], axis=1)
    parts = [
        *t["right"], *t["right_t"], t["ones"], t["left"][0], t["left_t"][0], t["back"][0],
        beside(t["left"][1], t["left_t"][1]), beside(t["back"][1], t["back"][1]), t["spread"],
    ]
    return jnp.asarray(np.concatenate(parts, axis=0))


def shards(grads, momentum, master, band_index):
    rows, cols = master.shape
    reps, _, lanes = band_index.shape
    groups = cols // GROUP
    dma = pltpu.SemaphoreType.DMA
    table = table_array()
    anywhere = pl.BlockSpec(memory_space=pl.ANY)
    vmem = pltpu.VMEM
    return tuple(pl.pallas_call(
        kernel,
        in_specs=[anywhere] * 5,
        out_specs=[anywhere] * 3,
        out_shape=[
            jax.ShapeDtypeStruct(momentum.shape, f32),
            jax.ShapeDtypeStruct(master.shape, f32),
            jax.ShapeDtypeStruct((rows, 4 * cols), bf16),
        ],
        scratch_shapes=[
            vmem((rows, cols), bf16),
            vmem((rows, cols), f32),
            vmem((groups * rows, GROUP), f32),
            vmem((groups * rows, BLOCK), bf16),
            vmem((2, lanes), jnp.int32),
            vmem((2, 4, 8, 2, lanes), jnp.int32),
            vmem((groups * 64, 128), jnp.int32),
            vmem((reps, groups, 128), f32),
            vmem((rows, cols), f32),
            vmem((rows, cols), f32),
            vmem((4, rows, cols), bf16),
            vmem(table.shape, bf16),
            dma((STEPS, 2)), dma((4,)), dma((STEPS,)),
            dma((7,)), dma((7,)), dma((3,)), dma((3,)), dma((4,)), dma((4,)),
            dma((UNITS,)), dma((UNITS, 3, 3)), dma((UNITS, 3, 3)), dma((UNITS, 3)), dma((UNITS, 3)),
            dma((UNITS, 7)), dma((UNITS, 7)), dma((UNITS, 2)), dma((UNITS, 2)), dma((UNITS, 5)), dma((UNITS, 5)),
        ],
        compiler_params=pltpu.CompilerParams(
            collective_id=0, has_side_effects=True, vmem_limit_bytes=VMEM_LIMIT
        ),
    )(grads, momentum, band_index.reshape(4, 8, 2, 2, lanes), master, table))


def solution(mesh):
    in_specs = (
        P("rep", None, "fsdp"),
        P("rep", None, "fsdp"),
        P(None, "fsdp"),
        P(None, None, "fsdp"),
    )
    out_specs = (P("rep", None, "fsdp"), P(None, "fsdp"), P())
    return jax.shard_map(shards, mesh=mesh, in_specs=in_specs, out_specs=out_specs, check_vma=False)
```

```python
import jax
import jax.numpy as jnp
import numpy as np
import ml_dtypes
from jax import lax
from jax.experimental import pallas as pl
from jax.experimental.pallas import tpu as pltpu
from jax.sharding import PartitionSpec as P

BLOCK = 64
BAND = 16
GROUP = 256
PER_STEP = 3

momentum_decay = 0.9
learn_rate = 0.05

bf16 = jnp.bfloat16
f32 = jnp.float32
MESH = pl.DeviceIdType.MESH
VMEM_LIMIT = 46 * 2**20


def dct64():
    k = np.arange(BLOCK, dtype=np.float64)[:, None]
    n = np.arange(BLOCK, dtype=np.float64)[None, :]
    basis = np.cos(np.pi * (2.0 * n + 1.0) * k / (2.0 * BLOCK))
    return basis * np.where(k == 0.0, np.sqrt(1.0 / BLOCK), np.sqrt(2.0 / BLOCK))


def halves(table):
    hi = table.astype(np.float32).astype(ml_dtypes.bfloat16)
    lo = (table - hi.astype(np.float64)).astype(np.float32).astype(ml_dtypes.bfloat16)
    return hi, lo


def left_pair(table):
    hi, lo = halves(table)
    return np.concatenate([hi, hi], axis=1), lo


def make_tables():
    c = dct64()
    right = np.kron(np.eye(4), c.T)
    left = np.kron(np.eye(2), c)
    m, i = np.divmod(np.arange(BLOCK), 8)
    k1 = 4 * (m + 8 * (i // 4)) + i % 4
    back_perm = np.kron(np.eye(2), c[k1].T)
    spread = np.kron(np.eye(4), np.ones((BAND, BLOCK)))
    ones = np.kron(np.eye(4), np.ones((BLOCK, BLOCK)))
    as_bf16 = lambda a: a.astype(ml_dtypes.bfloat16)
    return dict(
        right=halves(right),
        right_t=halves(right.T),
        left=left_pair(left),
        left_t=left_pair(left.T),
        back=left_pair(back_perm),
        spread=as_bf16(spread),
        ones=as_bf16(ones),
    )


TABLES = make_tables()


def split(x):
    hi = x.astype(bf16)
    return hi, (x - hi.astype(f32)).astype(bf16)


def dot(a, b):
    return jnp.dot(a, b, preferred_element_type=f32)


def dot_nt(a, b):
    return lax.dot_general(a, b, (((1,), (1,)), ((), ())), preferred_element_type=f32)


def times_right(x, hi_ref, lo_ref):
    hi, lo = split(x)
    return dot(hi, hi_ref[...]) + (dot(lo, hi_ref[...]) + dot(hi, lo_ref[...]))


def times_left(pair_ref, lo_ref, x):
    hi, lo = split(x)
    return dot(pair_ref[...], jnp.concatenate([hi, lo], axis=0)) + dot(lo_ref[...], hi)


def summed_coefficients(band, index):
    reps = band.shape[1] // 2
    half = jnp.where(lax.broadcasted_iota(jnp.int32, (8, 2 * reps), 1) >= reps, 4, 0)
    eight = lax.broadcasted_iota(jnp.int32, (8, 2 * reps), 0)
    k2_of = lax.broadcasted_iota(jnp.int32, (BLOCK, 2 * reps), 0)
    zero = jnp.zeros((8, 2 * reps), f32)
    quarter = lax.broadcasted_iota(jnp.int32, (16, GROUP), 1) >> 6
    parts = []
    for p in range(2):
        values, codes, places = [], [], []
        for q in range(4):
            base = (p * 4 + q) * 8
            w = index[base : base + 8]
            values.append(band[base : base + 8])
            codes.append((w >> 6) + half)
            places.append(w & 63)
        for t in range(4):
            his, los, hots = [], [], []
            for q in range(4):
                a, b = [], []
                for m in (2 * t, 2 * t + 1):
                    spread = lambda x: jnp.broadcast_to(x[m : m + 1], eight.shape)
                    a.append(jnp.where(spread(codes[q]) == eight, spread(values[q]), 0.0))
                    here = jnp.broadcast_to(places[q][m : m + 1], k2_of.shape) == k2_of
                    b.append(jnp.where(here, 1.0, 0.0).astype(bf16))
                left = jnp.concatenate(
                    [jnp.concatenate([a[0], zero], axis=1), jnp.concatenate([zero, a[1]], axis=1)], axis=0
                )
                hi, lo = split(left)
                his.append(hi)
                los.append(lo)
                hots.append(jnp.concatenate(b, axis=1))
            out = dot_nt(jnp.concatenate(his + los, axis=0), jnp.concatenate(hots, axis=0))
            out = out[:64] + out[64:]
            rows = jnp.where(quarter == 0, out[:16], 0.0)
            for q in range(1, 4):
                rows = jnp.where(quarter == q, out[16 * q : 16 * (q + 1)], rows)
            parts.append(rows)
    return jnp.concatenate(parts, axis=0)


def shared_group(band, index, master, rt_hi, rt_lo, b_pair, b_lo, ones_ref):
    total = summed_coefficients(band, index)
    direction = times_left(b_pair, b_lo, times_right(total, rt_hi, rt_lo))
    square = direction * direction
    sums = [
        jnp.broadcast_to(jnp.sum(square[p * BLOCK : (p + 1) * BLOCK], axis=0, keepdims=True), (8, GROUP))
        for p in range(2)
    ]
    hi, lo = split(jnp.concatenate(sums, axis=0))
    means = (dot(hi, ones_ref[...]) + dot(lo, ones_ref[...])) * (1.0 / (BLOCK * BLOCK))
    scale = 0.1 * jnp.sqrt(means + 1e-06)
    scale = jnp.concatenate(
        [jnp.broadcast_to(scale[8 * p : 8 * p + 1], (BLOCK, GROUP)) for p in range(2)], axis=0
    )
    update = direction / (jnp.abs(direction) + scale)
    return update, (master - learn_rate * update).astype(bf16)


def rep_parts(r):
    return r // 16, (r // 2) % 8, r % 2


def rep_of(x, z, core):
    return x * 16 + z * 2 + core


UNITS = 7
WIDE = 2 * GROUP
Y_AFTER, ONWARD_AFTER, SWAP_AFTER = 2, 4, 6
STEPS = 9
EARLY, MIDDLE = 2, 6


def kernel(
    grads_ref, mom_ref, index_ref, master_ref, table_ref,
    acc, updates, slots,
    grads, kept_rows, wide, own_index, index_rows, places, rows, masters, table,
    in_sem, index_sem, gz_send, gz_recv, gx_send, gx_recv, gs_send, gs_recv,
    m_sem, y_send, y_recv, x_send, x_recv, z_send, z_recv, s_send, s_recv,
):
    rep = lax.axis_index("rep")
    shard = lax.axis_index("fsdp")
    x, z, core = rep_parts(rep)
    cols = masters.shape[1]
    groups = cols // GROUP
    sibling = rep_of(x, z, 1 - core)
    y_peers = [lax.rem(shard + d, 4) for d in range(1, 4)]
    x_peers = [rep_of(lax.rem(x + d, 4), z, core) for d in range(1, 4)]
    z_peers = [rep_of(x, lax.rem(z + d, 8), core) for d in range(1, 8)]
    chunk = PER_STEP * GROUP
    tall = PER_STEP * 2 * BLOCK

    def remote(src, dst, send, recv, peer):
        return pltpu.make_async_remote_copy(
            src_ref=src, dst_ref=dst, send_sem=send, recv_sem=recv, device_id=peer, device_id_type=MESH,
        )


    def columns(step):
        return pl.ds(pl.multiple_of(step * chunk, chunk), chunk)

    def in_copies(step):
        at = columns(step)
        return (
            pltpu.make_async_copy(grads_ref.at[0, :, at], grads.at[:, at], in_sem.at[step, 0]),
            pltpu.make_async_copy(mom_ref.at[0, :, at], acc.at[:, at], in_sem.at[step, 1]),
        )

    def first_group(of_core, unit):
        return 2 * unit + of_core * (groups - 2 - 4 * unit)

    def span(of_core, unit):
        return pl.ds(pl.multiple_of(first_group(of_core, unit) * GROUP, GROUP), WIDE)

    def last_span(of_core):
        return pl.ds(pl.multiple_of((groups // 2 - 1 + 2 * of_core) * GROUP, GROUP), GROUP)

    def master_copy(unit):
        at = span(core, unit)
        return pltpu.make_async_copy(master_ref.at[:, at], masters.at[:, at], m_sem.at[unit])

    pull_own = pltpu.make_async_copy(index_ref.at[x, z, core], own_index, index_sem.at[2])
    pull_table = pltpu.make_async_copy(table_ref, table, index_sem.at[3])
    pulls = [pltpu.make_async_copy(index_ref.at[:, :, c], index_rows.at[c], index_sem.at[c]) for c in range(2)]
    pull_own.start()
    pull_table.start()

    @pl.loop(0, STEPS)
    def _(step):
        for copy in in_copies(step):
            copy.start()

    for pull in pulls:
        pull.start()

    @pl.loop(0, UNITS)
    def _(unit):
        master_copy(unit).start()

    barrier = pltpu.get_barrier_semaphore()
    for peer in y_peers:
        pl.semaphore_signal(barrier, inc=1, device_id={"fsdp": peer}, device_id_type=MESH)
    for peer in x_peers + z_peers + [sibling]:
        pl.semaphore_signal(barrier, inc=1, device_id={"rep": peer}, device_id_type=MESH)


    r_hi, r_lo, rt_hi, rt_lo, ones = (table.at[k * 256 : (k + 1) * 256] for k in range(5))
    l_pair, lt_pair, b_pair = (table.at[1280 + k * 128 : 1408 + k * 128] for k in range(3))
    l_lo, lt_lo = (table.at[1664:1792, k * 128 : (k + 1) * 128] for k in range(2))
    b_lo = table.at[1792:1920, 0:128]
    spread_ref = table.at[1920:1984]

    pull_own.wait()
    row = lax.broadcasted_iota(jnp.int32, (BLOCK, groups * BLOCK), 0)
    lane = lax.broadcasted_iota(jnp.int32, (BLOCK, groups * BLOCK), 1)
    own_slot = (lane & (BAND - 1)) == (row >> 2)
    for p in range(2):
        within = own_index[p : p + 1, :] & 255
        placed = jnp.where(own_slot, jnp.broadcast_to(within, own_slot.shape), 0).astype(f32)
        for g in range(groups):
            at = (2 * g + p) * BLOCK
            wide[at : at + BLOCK, :] = placed[:, g * BLOCK : (g + 1) * BLOCK].astype(bf16)
    pull_table.wait()

    mine = core * 32 + x * 8 + z

    @pl.loop(0, STEPS)
    def _(step):
        for copy in in_copies(step):
            copy.wait()
        at = columns(step)
        total = momentum_decay * acc[:, at] + grads[:, at].astype(f32)
        acc[:, at] = total
        stacked = jnp.concatenate([total[:, g * GROUP : (g + 1) * GROUP] for g in range(PER_STEP)], axis=0)
        half = times_right(stacked, r_hi, r_lo)
        coeff = jnp.concatenate(
            [times_left(l_pair, l_lo, half[g * 128 : (g + 1) * 128]) for g in range(PER_STEP)], axis=0
        )
        tall_at = pl.ds(pl.multiple_of(step * tall, tall), tall)
        index = dot(wide[tall_at, :], spread_ref[...])
        row = lax.broadcasted_iota(jnp.int32, (tall, GROUP), 0)
        lane = lax.broadcasted_iota(jnp.int32, (tall, GROUP), 1)
        place = (((row & 3) << 6) + (lane & 63)).astype(f32)
        kept = jnp.where(index == place, coeff, 0.0)
        kept_rows[tall_at, :] = kept
        hi, mid = split(kept)
        sums = dot_nt(hi, spread_ref[...]) + dot_nt(mid, spread_ref[...])
        zrow = lax.broadcasted_iota(jnp.int32, (tall, BLOCK), 0)
        zlane = lax.broadcasted_iota(jnp.int32, (tall, BLOCK), 1)
        sums = jnp.where((zlane & (BAND - 1)) == ((zrow & 63) >> 2), sums, 0.0)
        for g in range(PER_STEP):
            pair = [
                jnp.sum(sums[(2 * g + p) * BLOCK : (2 * g + p + 1) * BLOCK], axis=0, keepdims=True)
                for p in range(2)
            ]
            rows[mine, pl.ds(step * PER_STEP + g, 1), :] = jnp.concatenate(pair, axis=1)

    def inverse_turn(step):
        half = times_right(kept_rows[pl.ds(pl.multiple_of(step * tall, tall), tall), :], rt_hi, rt_lo)
        for g in range(PER_STEP):
            at = pl.ds(pl.multiple_of(step * chunk + g * GROUP, GROUP), GROUP)
            acc[:, at] = acc[:, at] - times_left(lt_pair, lt_lo, half[g * 128 : (g + 1) * 128])


    pl.semaphore_wait(barrier, 14)
    own = rows.at[mine]
    gz = [remote(own, own, gz_send.at[d], gz_recv.at[d], {"rep": peer}) for d, peer in enumerate(z_peers)]
    for copy in gz:
        copy.start()

    for pull in pulls:
        pull.wait()
    for p in range(2):
        for k in range((groups + 1) // 2):
            lanes = min(128, groups * BLOCK - k * 128)
            part = index_rows[:, :, :, p, k * 128 : k * 128 + lanes].reshape(64, lanes)
            turned = part.T & 255
            for b in range(lanes // BAND):
                at = (((2 * k + b // 4) * 2 + p) * 4 + b % 4) * 8
                places[at : at + 8, :] = jnp.concatenate(
                    [turned[b * 16 : b * 16 + 8], turned[b * 16 + 8 : b * 16 + 16]], axis=1
                )
    pl.loop(0, EARLY)(inverse_turn)

    for copy in gz:
        copy.wait()

    def bundle(of_x):
        return rows.at[pl.ds(core * 32 + of_x * 8, 8)]

    gx = [remote(bundle(x), bundle(x), gx_send.at[d], gx_recv.at[d], {"rep": peer}) for d, peer in enumerate(x_peers)]
    for copy in gx:
        copy.start()
    gs = [remote(bundle(x), bundle(x), gs_send.at[0], gs_recv.at[0], {"rep": sibling})]
    gs[0].start()
    pl.loop(EARLY, MIDDLE)(inverse_turn)
    for d in range(1, 4):
        gx[d - 1].wait_recv()
        part = bundle(lax.rem(x + 4 - d, 4))
        copy = remote(part, part, gs_send.at[d], gs_recv.at[d], {"rep": sibling})
        copy.start()
        gs.append(copy)
    for copy in gx:
        copy.wait_send()
    for copy in gs:
        copy.wait()


    def y_copies(unit):
        at = span(core, unit)
        parts = (
            (pl.ds(0, 32), at),
            (x_rows(x), at),
            z_part(z, unit),
        )
        return [
            remote(
                slots.at[0, rows_at, cols_at], slots.at[d + 1, rows_at, cols_at],
                y_send.at[unit, d, k], y_recv.at[unit, d, k], {"fsdp": y_peers[d]},
            )
            for d in range(3)
            for k, (rows_at, cols_at) in enumerate(parts)
        ]

    def x_rows(of_x):
        return pl.ds(pl.multiple_of(32 + of_x * 16, 16), 16)

    def z_part(of_z, unit):
        start = first_group(core, unit) * GROUP + (of_z % 4) * 128
        return pl.ds(pl.multiple_of(96 + (of_z // 4) * 16, 16), 16), pl.ds(pl.multiple_of(start, 128), 128)

    def onward_copies(unit, arriving):
        at = span(core, unit)
        out = []
        for d in range(3):
            part = slots.at[pl.ds(1, 3), x_rows(lax.rem(x + 3 - d, 4) if arriving else x), at]
            out.append(remote(part, part, x_send.at[unit, d], x_recv.at[unit, d], {"rep": x_peers[d]}))
        for d in range(7):
            rows_at, cols_at = z_part(lax.rem(z + 7 - d, 8) if arriving else z, unit)
            part = slots.at[pl.ds(1, 3), rows_at, cols_at]
            out.append(remote(part, part, z_send.at[unit, d], z_recv.at[unit, d], {"rep": z_peers[d]}))
        return out

    def s_copies(unit, at):
        return [
            remote(part, part, s_send.at[unit, k], s_recv.at[unit, k], {"rep": sibling})
            for k, part in enumerate((slots.at[:, :, at], updates.at[:, at]))
        ]

    def by_width(of_core, unit, act):
        @pl.when(unit < UNITS - 1)
        def _():
            act(span(of_core, unit))

        @pl.when(unit == UNITS - 1)
        def _():
            act(last_span(of_core))

    tables = (rt_hi, rt_lo, b_pair, b_lo, ones)

    @pl.loop(0, UNITS + SWAP_AFTER)
    def _(step):
        @pl.when(step < UNITS)
        def _():
            master_copy(step).wait()
            for k in range(2):
                g = first_group(core, step) + k
                turned = rows[:, g, :].T
                band = jnp.concatenate(
                    [
                        jnp.concatenate([turned[b * 16 : b * 16 + 8], turned[b * 16 + 8 : b * 16 + 16]], axis=1)
                        for b in range(8)
                    ],
                    axis=0,
                )
                lanes = pl.ds(pl.multiple_of(g * 64, 64), 64)
                at = pl.ds(pl.multiple_of(g * GROUP, GROUP), GROUP)
                update, weights = shared_group(band, places[lanes, :], masters[:, at], *tables)
                updates[:, at] = update
                slots[0, :, at] = weights
            for copy in y_copies(step):
                copy.start()

        @pl.when((step >= Y_AFTER) & (step < UNITS + Y_AFTER))
        def _():
            for copy in y_copies(step - Y_AFTER):
                copy.wait_recv()
            for copy in onward_copies(step - Y_AFTER, False):
                copy.start()

        @pl.when((step >= UNITS) & (step < UNITS + STEPS - MIDDLE))
        def _():
            inverse_turn(MIDDLE + step - UNITS)

        @pl.when((step >= ONWARD_AFTER) & (step < UNITS + ONWARD_AFTER))
        def _():
            unit = step - ONWARD_AFTER
            for copy in onward_copies(unit, True):
                copy.wait_recv()

            def act(at):
                for copy in s_copies(unit, at):
                    copy.start()

            by_width(core, unit, act)

        @pl.when(step >= SWAP_AFTER)
        def _():
            unit = step - SWAP_AFTER

            def act(at):
                for copy in s_copies(unit, at):
                    copy.wait_recv()

            by_width(1 - core, unit, act)

    @pl.loop(0, UNITS)
    def _(unit):
        for copy in y_copies(unit) + onward_copies(unit, False):
            copy.wait_send()

        def drain_own(at):
            for copy in s_copies(unit, at):
                copy.wait_send()

        by_width(core, unit, drain_own)


def table_array():
    t = TABLES
    beside = lambda a, b: np.concatenate([a, b], axis=1)
    parts = [
        *t["right"], *t["right_t"], t["ones"], t["left"][0], t["left_t"][0], t["back"][0],
        beside(t["left"][1], t["left_t"][1]), beside(t["back"][1], t["back"][1]), t["spread"],
    ]
    return jnp.asarray(np.concatenate(parts, axis=0))


def settle(fresh, update, slots):
    rows, cols = update.shape
    part = cols // 9

    def body(fresh_ref, update_ref, slots_ref, fresh_out, update_out, weights_out, sem):
        shard = lax.axis_index("fsdp")
        copies = []
        for n in range(9):
            at = slice(n * part, (n + 1) * part)
            copies.append(pltpu.make_async_copy(fresh_ref.at[:, at], fresh_out.at[0, :, at], sem.at[n, 0]))
            copies.append(pltpu.make_async_copy(update_ref.at[:, at], update_out.at[:, at], sem.at[n, 1]))
        for d in range(4):
            from_shard = lax.rem(shard + 4 - d, 4)
            for n in range(3):
                start = pl.multiple_of(from_shard * cols + n * 3 * part, GROUP)
                copies.append(pltpu.make_async_copy(
                    slots_ref.at[d, :, n * 3 * part : (n + 1) * 3 * part],
                    weights_out.at[:, pl.ds(start, 3 * part)],
                    sem.at[d * 3 + n, 2],
                ))
        for copy in copies:
            copy.start()
        for copy in copies:
            copy.wait()

    anywhere = pl.BlockSpec(memory_space=pl.ANY)
    return tuple(pl.pallas_call(
        body,
        in_specs=[anywhere] * 3,
        out_specs=[anywhere] * 3,
        out_shape=[
            jax.ShapeDtypeStruct((1, rows, cols), f32),
            jax.ShapeDtypeStruct((rows, cols), f32),
            jax.ShapeDtypeStruct((rows, 4 * cols), bf16),
        ],
        scratch_shapes=[pltpu.SemaphoreType.DMA((12, 3))],
        compiler_params=pltpu.CompilerParams(vmem_limit_bytes=2 * 2**20),
    )(fresh, update, slots))


def shards(grads, momentum, master, band_index):
    rows, cols = master.shape
    reps, _, lanes = band_index.shape
    groups = cols // GROUP
    dma = pltpu.SemaphoreType.DMA
    table = table_array()
    anywhere = pl.BlockSpec(memory_space=pl.ANY)
    vmem = pltpu.VMEM
    return settle(*pl.pallas_call(
        kernel,
        in_specs=[anywhere] * 5,
        out_specs=[pl.BlockSpec(memory_space=vmem)] * 3,
        out_shape=[vmem((rows, cols), f32), vmem((rows, cols), f32), vmem((4, rows, cols), bf16)],
        scratch_shapes=[
            vmem((rows, cols), bf16),
            vmem((groups * rows, GROUP), f32),
            vmem((groups * rows, BLOCK), bf16),
            vmem((2, lanes), jnp.int32),
            vmem((2, 4, 8, 2, lanes), jnp.int32),
            vmem((groups * 64, 128), jnp.int32),
            vmem((reps, groups, 128), f32),
            vmem((rows, cols), f32),
            vmem(table.shape, bf16),
            dma((STEPS, 2)), dma((4,)),
            dma((7,)), dma((7,)), dma((3,)), dma((3,)), dma((4,)), dma((4,)),
            dma((UNITS,)), dma((UNITS, 3, 3)), dma((UNITS, 3, 3)), dma((UNITS, 3)), dma((UNITS, 3)),
            dma((UNITS, 7)), dma((UNITS, 7)), dma((UNITS, 2)), dma((UNITS, 2)),
        ],
        compiler_params=pltpu.CompilerParams(
            collective_id=0, has_side_effects=True, vmem_limit_bytes=VMEM_LIMIT
        ),
    )(grads, momentum, band_index.reshape(4, 8, 2, 2, lanes), master, table))


def solution(mesh):
    in_specs = (
        P("rep", None, "fsdp"),
        P("rep", None, "fsdp"),
        P(None, "fsdp"),
        P(None, None, "fsdp"),
    )
    out_specs = (P("rep", None, "fsdp"), P(None, "fsdp"), P())
    return jax.shard_map(shards, mesh=mesh, in_specs=in_specs, out_specs=out_specs, check_vma=False)
```

```python
import jax
import jax.numpy as jnp
import numpy as np
import ml_dtypes
from jax import lax
from jax.experimental import pallas as pl
from jax.experimental.pallas import tpu as pltpu
from jax.sharding import PartitionSpec as P

BLOCK = 64
BAND = 16
GROUP = 256
PER_STEP = 3

momentum_decay = 0.9
learn_rate = 0.05

bf16 = jnp.bfloat16
f32 = jnp.float32
MESH = pl.DeviceIdType.MESH
VMEM_LIMIT = 46 * 2**20


def dct64():
    k = np.arange(BLOCK, dtype=np.float64)[:, None]
    n = np.arange(BLOCK, dtype=np.float64)[None, :]
    basis = np.cos(np.pi * (2.0 * n + 1.0) * k / (2.0 * BLOCK))
    return basis * np.where(k == 0.0, np.sqrt(1.0 / BLOCK), np.sqrt(2.0 / BLOCK))


def halves(table):
    hi = table.astype(np.float32).astype(ml_dtypes.bfloat16)
    lo = (table - hi.astype(np.float64)).astype(np.float32).astype(ml_dtypes.bfloat16)
    return hi, lo


def left_pair(table):
    hi, lo = halves(table)
    return np.concatenate([hi, hi], axis=1), lo


def make_tables():
    c = dct64()
    right = np.kron(np.eye(4), c.T)
    left = np.kron(np.eye(2), c)
    m, i = np.divmod(np.arange(BLOCK), 8)
    k1 = 4 * (m + 8 * (i // 4)) + i % 4
    back_perm = np.kron(np.eye(2), c[k1].T)
    spread = np.kron(np.eye(4), np.ones((BAND, BLOCK)))
    ones = np.kron(np.eye(4), np.ones((BLOCK, BLOCK)))
    as_bf16 = lambda a: a.astype(ml_dtypes.bfloat16)
    return dict(
        right=halves(right),
        right_t=halves(right.T),
        left=left_pair(left),
        left_t=left_pair(left.T),
        back=left_pair(back_perm),
        spread=as_bf16(spread),
        ones=as_bf16(ones),
    )


TABLES = make_tables()


def split(x):
    hi = x.astype(bf16)
    return hi, (x - hi.astype(f32)).astype(bf16)


def dot(a, b):
    return jnp.dot(a, b, preferred_element_type=f32)


def dot_nt(a, b):
    return lax.dot_general(a, b, (((1,), (1,)), ((), ())), preferred_element_type=f32)


def times_right(x, hi_ref, lo_ref):
    hi, lo = split(x)
    return dot(hi, hi_ref[...]) + (dot(lo, hi_ref[...]) + dot(hi, lo_ref[...]))


def times_left(pair_ref, lo_ref, x):
    hi, lo = split(x)
    return dot(pair_ref[...], jnp.concatenate([hi, lo], axis=0)) + dot(lo_ref[...], hi)


def summed_coefficients(band, index):
    reps = band.shape[1] // 2
    half = jnp.where(lax.broadcasted_iota(jnp.int32, (8, 2 * reps), 1) >= reps, 4, 0)
    eight = lax.broadcasted_iota(jnp.int32, (8, 2 * reps), 0)
    k2_of = lax.broadcasted_iota(jnp.int32, (BLOCK, 2 * reps), 0)
    zero = jnp.zeros((8, 2 * reps), f32)
    quarter = lax.broadcasted_iota(jnp.int32, (16, GROUP), 1) >> 6
    parts = []
    for p in range(2):
        values, codes, places = [], [], []
        for q in range(4):
            base = (p * 4 + q) * 8
            w = index[base : base + 8]
            values.append(band[base : base + 8])
            codes.append((w >> 6) + half)
            places.append(w & 63)
        for t in range(4):
            his, los, hots = [], [], []
            for q in range(4):
                a, b = [], []
                for m in (2 * t, 2 * t + 1):
                    spread = lambda x: jnp.broadcast_to(x[m : m + 1], eight.shape)
                    a.append(jnp.where(spread(codes[q]) == eight, spread(values[q]), 0.0))
                    here = jnp.broadcast_to(places[q][m : m + 1], k2_of.shape) == k2_of
                    b.append(jnp.where(here, 1.0, 0.0).astype(bf16))
                left = jnp.concatenate(
                    [jnp.concatenate([a[0], zero], axis=1), jnp.concatenate([zero, a[1]], axis=1)], axis=0
                )
                hi, lo = split(left)
                his.append(hi)
                los.append(lo)
                hots.append(jnp.concatenate(b, axis=1))
            out = dot_nt(jnp.concatenate(his + los, axis=0), jnp.concatenate(hots, axis=0))
            out = out[:64] + out[64:]
            rows = jnp.where(quarter == 0, out[:16], 0.0)
            for q in range(1, 4):
                rows = jnp.where(quarter == q, out[16 * q : 16 * (q + 1)], rows)
            parts.append(rows)
    return jnp.concatenate(parts, axis=0)


def shared_group(band, index, master, rt_hi, rt_lo, b_pair, b_lo, ones_ref):
    total = summed_coefficients(band, index)
    direction = times_left(b_pair, b_lo, times_right(total, rt_hi, rt_lo))
    square = direction * direction
    sums = [
        jnp.broadcast_to(jnp.sum(square[p * BLOCK : (p + 1) * BLOCK], axis=0, keepdims=True), (8, GROUP))
        for p in range(2)
    ]
    hi, lo = split(jnp.concatenate(sums, axis=0))
    means = (dot(hi, ones_ref[...]) + dot(lo, ones_ref[...])) * (1.0 / (BLOCK * BLOCK))
    scale = 0.1 * jnp.sqrt(means + 1e-06)
    scale = jnp.concatenate(
        [jnp.broadcast_to(scale[8 * p : 8 * p + 1], (BLOCK, GROUP)) for p in range(2)], axis=0
    )
    update = direction / (jnp.abs(direction) + scale)
    return update, (master - learn_rate * update).astype(bf16)


def sent_place(g):
    from_8, from_19 = (g + 24) // 32, (g + 5) // 24
    return g + 8 * from_8 + from_19 * (26 - 2 * g)


def rep_parts(r):
    return r // 16, (r // 2) % 8, r % 2


def rep_of(x, z, core):
    return x * 16 + z * 2 + core


UNITS = 7
WIDE = 2 * GROUP
Y_AFTER, ONWARD_AFTER, SWAP_AFTER = 2, 4, 6
STEPS = 9
EARLY, MIDDLE = 2, 6


def kernel(
    grads_ref, mom_ref, index_ref, master_ref, table_ref,
    acc, updates, slots,
    grads, kept_rows, wide, own_index, index_rows, places, rows, masters, table,
    in_sem, index_sem, gz_send, gz_recv, gx_send, gx_recv, gs_send, gs_recv,
    m_sem, y_send, y_recv, x_send, x_recv, z_send, z_recv, s_send, s_recv,
):
    rep = lax.axis_index("rep")
    shard = lax.axis_index("fsdp")
    x, z, core = rep_parts(rep)
    cols = masters.shape[1]
    groups = cols // GROUP
    sibling = rep_of(x, z, 1 - core)
    y_peers = [lax.rem(shard + d, 4) for d in range(1, 4)]
    x_peers = [rep_of(lax.rem(x + d, 4), z, core) for d in range(1, 4)]
    z_peers = [rep_of(x, lax.rem(z + d, 8), core) for d in range(1, 8)]
    chunk = PER_STEP * GROUP
    tall = PER_STEP * 2 * BLOCK

    def remote(src, dst, send, recv, peer):
        return pltpu.make_async_remote_copy(
            src_ref=src, dst_ref=dst, send_sem=send, recv_sem=recv, device_id=peer, device_id_type=MESH,
        )


    def columns(step):
        return pl.ds(pl.multiple_of(step * chunk, chunk), chunk)

    def in_copies(step):
        at = columns(step)
        return (
            pltpu.make_async_copy(grads_ref.at[0, :, at], grads.at[:, at], in_sem.at[step, 0]),
            pltpu.make_async_copy(mom_ref.at[0, :, at], acc.at[:, at], in_sem.at[step, 1]),
        )

    def first_group(of_core, unit):
        return 2 * unit + of_core * (groups - 2 - 4 * unit)

    def span(of_core, unit):
        return pl.ds(pl.multiple_of(first_group(of_core, unit) * GROUP, GROUP), WIDE)

    def last_span(of_core):
        return pl.ds(pl.multiple_of((groups // 2 - 1 + 2 * of_core) * GROUP, GROUP), GROUP)

    def master_copy(unit):
        at = span(core, unit)
        return pltpu.make_async_copy(master_ref.at[:, at], masters.at[:, at], m_sem.at[unit])

    pull_own = pltpu.make_async_copy(index_ref.at[x, z, core], own_index, index_sem.at[2])
    pull_table = pltpu.make_async_copy(table_ref, table, index_sem.at[3])
    pulls = [pltpu.make_async_copy(index_ref.at[:, :, c], index_rows.at[c], index_sem.at[c]) for c in range(2)]
    pull_own.start()
    pull_table.start()

    @pl.loop(0, STEPS)
    def _(step):
        for copy in in_copies(step):
            copy.start()

    for pull in pulls:
        pull.start()

    @pl.loop(0, UNITS)
    def _(unit):
        master_copy(unit).start()

    barrier = pltpu.get_barrier_semaphore()
    for peer in y_peers:
        pl.semaphore_signal(barrier, inc=1, device_id={"fsdp": peer}, device_id_type=MESH)
    for peer in x_peers + z_peers + [sibling]:
        pl.semaphore_signal(barrier, inc=1, device_id={"rep": peer}, device_id_type=MESH)


    r_hi, r_lo, rt_hi, rt_lo, ones = (table.at[k * 256 : (k + 1) * 256] for k in range(5))
    l_pair, lt_pair, b_pair = (table.at[1280 + k * 128 : 1408 + k * 128] for k in range(3))
    l_lo, lt_lo = (table.at[1664:1792, k * 128 : (k + 1) * 128] for k in range(2))
    b_lo = table.at[1792:1920, 0:128]
    spread_ref = table.at[1920:1984]

    pull_own.wait()
    row = lax.broadcasted_iota(jnp.int32, (BLOCK, groups * BLOCK), 0)
    lane = lax.broadcasted_iota(jnp.int32, (BLOCK, groups * BLOCK), 1)
    own_slot = (lane & (BAND - 1)) == (row >> 2)
    for p in range(2):
        within = own_index[p : p + 1, :] & 255
        placed = jnp.where(own_slot, jnp.broadcast_to(within, own_slot.shape), 0).astype(f32)
        for g in range(groups):
            at = (2 * g + p) * BLOCK
            wide[at : at + BLOCK, :] = placed[:, g * BLOCK : (g + 1) * BLOCK].astype(bf16)
    pull_table.wait()

    mine = core * 32 + x * 8 + z

    @pl.loop(0, STEPS)
    def _(step):
        for copy in in_copies(step):
            copy.wait()
        at = columns(step)
        total = momentum_decay * acc[:, at] + grads[:, at].astype(f32)
        acc[:, at] = total
        stacked = jnp.concatenate([total[:, g * GROUP : (g + 1) * GROUP] for g in range(PER_STEP)], axis=0)
        half = times_right(stacked, r_hi, r_lo)
        coeff = jnp.concatenate(
            [times_left(l_pair, l_lo, half[g * 128 : (g + 1) * 128]) for g in range(PER_STEP)], axis=0
        )
        tall_at = pl.ds(pl.multiple_of(step * tall, tall), tall)
        index = dot(wide[tall_at, :], spread_ref[...])
        row = lax.broadcasted_iota(jnp.int32, (tall, GROUP), 0)
        lane = lax.broadcasted_iota(jnp.int32, (tall, GROUP), 1)
        place = (((row & 3) << 6) + (lane & 63)).astype(f32)
        kept = jnp.where(index == place, coeff, 0.0)
        kept_rows[tall_at, :] = kept
        hi, mid = split(kept)
        sums = dot_nt(hi, spread_ref[...]) + dot_nt(mid, spread_ref[...])
        zrow = lax.broadcasted_iota(jnp.int32, (tall, BLOCK), 0)
        zlane = lax.broadcasted_iota(jnp.int32, (tall, BLOCK), 1)
        sums = jnp.where((zlane & (BAND - 1)) == ((zrow & 63) >> 2), sums, 0.0)
        for g in range(PER_STEP):
            pair = [
                jnp.sum(sums[(2 * g + p) * BLOCK : (2 * g + p + 1) * BLOCK], axis=0, keepdims=True)
                for p in range(2)
            ]
            rows[mine, pl.ds(sent_place(step * PER_STEP + g), 1), :] = jnp.concatenate(pair, axis=1)

    def inverse_turn(step):
        half = times_right(kept_rows[pl.ds(pl.multiple_of(step * tall, tall), tall), :], rt_hi, rt_lo)
        for g in range(PER_STEP):
            at = pl.ds(pl.multiple_of(step * chunk + g * GROUP, GROUP), GROUP)
            acc[:, at] = acc[:, at] - times_left(lt_pair, lt_lo, half[g * 128 : (g + 1) * 128])


    pl.semaphore_wait(barrier, 14)
    halves_at = (pl.ds(0, 16), pl.ds(16, groups - 16))

    def z_band_copies(h):
        own = rows.at[mine, halves_at[h]]
        return [
            remote(own, own, gz_send.at[h, d], gz_recv.at[h, d], {"rep": peer}) for d, peer in enumerate(z_peers)
        ]

    def bundle(of_x, h):
        return rows.at[pl.ds(core * 32 + of_x * 8, 8), halves_at[h]]

    def x_band_copies(h):
        part = bundle(x, h)
        return [
            remote(part, part, gx_send.at[h, d], gx_recv.at[h, d], {"rep": peer}) for d, peer in enumerate(x_peers)
        ]

    def s_band_copy(h, d):
        part = bundle(lax.rem(x + 4 - d, 4), h)
        return remote(part, part, gs_send.at[h, d], gs_recv.at[h, d], {"rep": sibling})

    def pass_on(h):
        for d, copy in enumerate(x_band_copies(h)):
            copy.wait_recv()
            s_band_copy(h, d + 1).start()

    for h in range(2):
        for copy in z_band_copies(h):
            copy.start()

    for pull in pulls:
        pull.wait()
    for p in range(2):
        for k in range((groups + 1) // 2):
            lanes = min(128, groups * BLOCK - k * 128)
            part = index_rows[:, :, :, p, k * 128 : k * 128 + lanes].reshape(64, lanes)
            turned = part.T & 255
            for b in range(lanes // BAND):
                at = (((2 * k + b // 4) * 2 + p) * 4 + b % 4) * 8
                places[at : at + 8, :] = jnp.concatenate(
                    [turned[b * 16 : b * 16 + 8], turned[b * 16 + 8 : b * 16 + 16]], axis=1
                )
    pl.loop(0, EARLY)(inverse_turn)

    for h in range(2):
        for copy in z_band_copies(h):
            copy.wait()
        for copy in x_band_copies(h):
            copy.start()
        s_band_copy(h, 0).start()
    pl.loop(EARLY, MIDDLE)(inverse_turn)
    pass_on(0)
    for d in range(4):
        s_band_copy(0, d).wait()


    def y_copies(unit):
        at = span(core, unit)
        parts = (
            (pl.ds(0, 32), at),
            (x_rows(x), at),
            z_part(z, unit),
        )
        return [
            remote(
                slots.at[0, rows_at, cols_at], slots.at[d + 1, rows_at, cols_at],
                y_send.at[unit, d, k], y_recv.at[unit, d, k], {"fsdp": y_peers[d]},
            )
            for d in range(3)
            for k, (rows_at, cols_at) in enumerate(parts)
        ]

    def x_rows(of_x):
        return pl.ds(pl.multiple_of(32 + of_x * 16, 16), 16)

    def z_part(of_z, unit):
        start = first_group(core, unit) * GROUP + (of_z % 4) * 128
        return pl.ds(pl.multiple_of(96 + (of_z // 4) * 16, 16), 16), pl.ds(pl.multiple_of(start, 128), 128)

    def onward_copies(unit, arriving):
        at = span(core, unit)
        out = []
        for d in range(3):
            part = slots.at[pl.ds(1, 3), x_rows(lax.rem(x + 3 - d, 4) if arriving else x), at]
            out.append(remote(part, part, x_send.at[unit, d], x_recv.at[unit, d], {"rep": x_peers[d]}))
        for d in range(7):
            rows_at, cols_at = z_part(lax.rem(z + 7 - d, 8) if arriving else z, unit)
            part = slots.at[pl.ds(1, 3), rows_at, cols_at]
            out.append(remote(part, part, z_send.at[unit, d], z_recv.at[unit, d], {"rep": z_peers[d]}))
        return out

    def s_copies(unit, at):
        return [
            remote(part, part, s_send.at[unit, k], s_recv.at[unit, k], {"rep": sibling})
            for k, part in enumerate((slots.at[:, :, at], updates.at[:, at]))
        ]

    def by_width(of_core, unit, act):
        @pl.when(unit < UNITS - 1)
        def _():
            act(span(of_core, unit))

        @pl.when(unit == UNITS - 1)
        def _():
            act(last_span(of_core))

    tables = (rt_hi, rt_lo, b_pair, b_lo, ones)

    @pl.loop(0, UNITS + SWAP_AFTER)
    def _(step):
        @pl.when(step == 1)
        def _():
            pass_on(1)

        @pl.when(step == 4)
        def _():
            for d in range(4):
                s_band_copy(1, d).wait()

        @pl.when(step < UNITS)
        def _():
            master_copy(step).wait()
            later = step // 4
            for k in range(2):
                g = first_group(core, step) + k
                early_place = 2 * step + k + core * (9 - 2 * k)
                turned = rows[:, (1 - later) * early_place + later * (g + 8), :].T
                band = jnp.concatenate(
                    [
                        jnp.concatenate([turned[b * 16 : b * 16 + 8], turned[b * 16 + 8 : b * 16 + 16]], axis=1)
                        for b in range(8)
                    ],
                    axis=0,
                )
                lanes = pl.ds(pl.multiple_of(g * 64, 64), 64)
                at = pl.ds(pl.multiple_of(g * GROUP, GROUP), GROUP)
                update, weights = shared_group(band, places[lanes, :], masters[:, at], *tables)
                updates[:, at] = update
                slots[0, :, at] = weights
            for copy in y_copies(step):
                copy.start()

        @pl.when((step >= Y_AFTER) & (step < UNITS + Y_AFTER))
        def _():
            for copy in y_copies(step - Y_AFTER):
                copy.wait_recv()
            for copy in onward_copies(step - Y_AFTER, False):
                copy.start()

        @pl.when((step >= UNITS) & (step < UNITS + STEPS - MIDDLE))
        def _():
            inverse_turn(MIDDLE + step - UNITS)

        @pl.when((step >= ONWARD_AFTER) & (step < UNITS + ONWARD_AFTER))
        def _():
            unit = step - ONWARD_AFTER
            for copy in onward_copies(unit, True):
                copy.wait_recv()

            def act(at):
                for copy in s_copies(unit, at):
                    copy.start()

            by_width(core, unit, act)

        @pl.when(step >= SWAP_AFTER)
        def _():
            unit = step - SWAP_AFTER

            def act(at):
                for copy in s_copies(unit, at):
                    copy.wait_recv()

            by_width(1 - core, unit, act)

    for h in range(2):
        for copy in x_band_copies(h):
            copy.wait_send()

    @pl.loop(0, UNITS)
    def _(unit):
        for copy in y_copies(unit) + onward_copies(unit, False):
            copy.wait_send()

        def drain_own(at):
            for copy in s_copies(unit, at):
                copy.wait_send()

        by_width(core, unit, drain_own)


def table_array():
    t = TABLES
    beside = lambda a, b: np.concatenate([a, b], axis=1)
    parts = [
        *t["right"], *t["right_t"], t["ones"], t["left"][0], t["left_t"][0], t["back"][0],
        beside(t["left"][1], t["left_t"][1]), beside(t["back"][1], t["back"][1]), t["spread"],
    ]
    return jnp.asarray(np.concatenate(parts, axis=0))


def settle(fresh, update, slots):
    rows, cols = update.shape
    part = cols // 9

    def body(fresh_ref, update_ref, slots_ref, fresh_out, update_out, weights_out, sem):
        shard = lax.axis_index("fsdp")
        copies = []
        for n in range(9):
            at = slice(n * part, (n + 1) * part)
            copies.append(pltpu.make_async_copy(fresh_ref.at[:, at], fresh_out.at[0, :, at], sem.at[n, 0]))
            copies.append(pltpu.make_async_copy(update_ref.at[:, at], update_out.at[:, at], sem.at[n, 1]))
        for d in range(4):
            from_shard = lax.rem(shard + 4 - d, 4)
            for n in range(3):
                start = pl.multiple_of(from_shard * cols + n * 3 * part, GROUP)
                copies.append(pltpu.make_async_copy(
                    slots_ref.at[d, :, n * 3 * part : (n + 1) * 3 * part],
                    weights_out.at[:, pl.ds(start, 3 * part)],
                    sem.at[d * 3 + n, 2],
                ))
        for copy in copies:
            copy.start()
        for copy in copies:
            copy.wait()

    anywhere = pl.BlockSpec(memory_space=pl.ANY)
    return tuple(pl.pallas_call(
        body,
        in_specs=[anywhere] * 3,
        out_specs=[anywhere] * 3,
        out_shape=[
            jax.ShapeDtypeStruct((1, rows, cols), f32),
            jax.ShapeDtypeStruct((rows, cols), f32),
            jax.ShapeDtypeStruct((rows, 4 * cols), bf16),
        ],
        scratch_shapes=[pltpu.SemaphoreType.DMA((12, 3))],
        compiler_params=pltpu.CompilerParams(vmem_limit_bytes=2 * 2**20),
    )(fresh, update, slots))


def shards(grads, momentum, master, band_index):
    rows, cols = master.shape
    reps, _, lanes = band_index.shape
    groups = cols // GROUP
    dma = pltpu.SemaphoreType.DMA
    table = table_array()
    anywhere = pl.BlockSpec(memory_space=pl.ANY)
    vmem = pltpu.VMEM
    return settle(*pl.pallas_call(
        kernel,
        in_specs=[anywhere] * 5,
        out_specs=[pl.BlockSpec(memory_space=vmem)] * 3,
        out_shape=[vmem((rows, cols), f32), vmem((rows, cols), f32), vmem((4, rows, cols), bf16)],
        scratch_shapes=[
            vmem((rows, cols), bf16),
            vmem((groups * rows, GROUP), f32),
            vmem((groups * rows, BLOCK), bf16),
            vmem((2, lanes), jnp.int32),
            vmem((2, 4, 8, 2, lanes), jnp.int32),
            vmem((groups * 64, 128), jnp.int32),
            vmem((reps, groups, 128), f32),
            vmem((rows, cols), f32),
            vmem(table.shape, bf16),
            dma((STEPS, 2)), dma((4,)),
            dma((2, 7)), dma((2, 7)), dma((2, 3)), dma((2, 3)), dma((2, 4)), dma((2, 4)),
            dma((UNITS,)), dma((UNITS, 3, 3)), dma((UNITS, 3, 3)), dma((UNITS, 3)), dma((UNITS, 3)),
            dma((UNITS, 7)), dma((UNITS, 7)), dma((UNITS, 2)), dma((UNITS, 2)),
        ],
        compiler_params=pltpu.CompilerParams(
            collective_id=0, has_side_effects=True, vmem_limit_bytes=VMEM_LIMIT
        ),
    )(grads, momentum, band_index.reshape(4, 8, 2, 2, lanes), master, table))


def solution(mesh):
    in_specs = (
        P("rep", None, "fsdp"),
        P("rep", None, "fsdp"),
        P(None, "fsdp"),
        P(None, None, "fsdp"),
    )
    out_specs = (P("rep", None, "fsdp"), P(None, "fsdp"), P())
    return jax.shard_map(shards, mesh=mesh, in_specs=in_specs, out_specs=out_specs, check_vma=False)
```

```python
import jax
import jax.numpy as jnp
import numpy as np
import ml_dtypes
from jax import lax
from jax.experimental import pallas as pl
from jax.experimental.pallas import tpu as pltpu
from jax.sharding import PartitionSpec as P

BLOCK = 64
BAND = 16
GROUP = 256
PER_STEP = 3

momentum_decay = 0.9
learn_rate = 0.05

bf16 = jnp.bfloat16
f32 = jnp.float32
MESH = pl.DeviceIdType.MESH
VMEM_LIMIT = 46 * 2**20


def dct64():
    k = np.arange(BLOCK, dtype=np.float64)[:, None]
    n = np.arange(BLOCK, dtype=np.float64)[None, :]
    basis = np.cos(np.pi * (2.0 * n + 1.0) * k / (2.0 * BLOCK))
    return basis * np.where(k == 0.0, np.sqrt(1.0 / BLOCK), np.sqrt(2.0 / BLOCK))


def halves(table):
    hi = table.astype(np.float32).astype(ml_dtypes.bfloat16)
    lo = (table - hi.astype(np.float64)).astype(np.float32).astype(ml_dtypes.bfloat16)
    return hi, lo


def left_pair(table):
    hi, lo = halves(table)
    return np.concatenate([hi, hi], axis=1), lo


def make_tables():
    c = dct64()
    right = np.kron(np.eye(4), c.T)
    left = np.kron(np.eye(2), c)
    m, i = np.divmod(np.arange(BLOCK), 8)
    k1 = 4 * (m + 8 * (i // 4)) + i % 4
    back_perm = np.kron(np.eye(2), c[k1].T)
    spread = np.kron(np.eye(4), np.ones((BAND, BLOCK)))
    ones = np.kron(np.eye(4), np.ones((BLOCK, BLOCK)))
    as_bf16 = lambda a: a.astype(ml_dtypes.bfloat16)
    return dict(
        right=halves(right),
        right_t=halves(right.T),
        left=left_pair(left),
        left_t=left_pair(left.T),
        back=left_pair(back_perm),
        spread=as_bf16(spread),
        ones=as_bf16(ones),
    )


TABLES = make_tables()


def split(x):
    hi = x.astype(bf16)
    return hi, (x - hi.astype(f32)).astype(bf16)


def dot(a, b):
    return jnp.dot(a, b, preferred_element_type=f32)


def dot_nt(a, b):
    return lax.dot_general(a, b, (((1,), (1,)), ((), ())), preferred_element_type=f32)


def times_right(x, hi_ref, lo_ref):
    hi, lo = split(x)
    return dot(hi, hi_ref[...]) + (dot(lo, hi_ref[...]) + dot(hi, lo_ref[...]))


def times_left(pair_ref, lo_ref, x):
    hi, lo = split(x)
    return dot(pair_ref[...], jnp.concatenate([hi, lo], axis=0)) + dot(lo_ref[...], hi)


def summed_coefficients(band, index):
    reps = band.shape[1] // 2
    half = jnp.where(lax.broadcasted_iota(jnp.int32, (8, 2 * reps), 1) >= reps, 4, 0)
    eight = lax.broadcasted_iota(jnp.int32, (8, 2 * reps), 0)
    k2_of = lax.broadcasted_iota(jnp.int32, (BLOCK, 2 * reps), 0)
    zero = jnp.zeros((8, 2 * reps), f32)
    quarter = lax.broadcasted_iota(jnp.int32, (16, GROUP), 1) >> 6
    parts = []
    for p in range(2):
        values, codes, places = [], [], []
        for q in range(4):
            base = (p * 4 + q) * 8
            w = index[base : base + 8]
            values.append(band[base : base + 8])
            codes.append((w >> 6) + half)
            places.append(w & 63)
        for t in range(4):
            his, los, hots = [], [], []
            for q in range(4):
                a, b = [], []
                for m in (2 * t, 2 * t + 1):
                    spread = lambda x: jnp.broadcast_to(x[m : m + 1], eight.shape)
                    a.append(jnp.where(spread(codes[q]) == eight, spread(values[q]), 0.0))
                    here = jnp.broadcast_to(places[q][m : m + 1], k2_of.shape) == k2_of
                    b.append(jnp.where(here, 1.0, 0.0).astype(bf16))
                left = jnp.concatenate(
                    [jnp.concatenate([a[0], zero], axis=1), jnp.concatenate([zero, a[1]], axis=1)], axis=0
                )
                hi, lo = split(left)
                his.append(hi)
                los.append(lo)
                hots.append(jnp.concatenate(b, axis=1))
            out = dot_nt(jnp.concatenate(his + los, axis=0), jnp.concatenate(hots, axis=0))
            out = out[:64] + out[64:]
            rows = jnp.where(quarter == 0, out[:16], 0.0)
            for q in range(1, 4):
                rows = jnp.where(quarter == q, out[16 * q : 16 * (q + 1)], rows)
            parts.append(rows)
    return jnp.concatenate(parts, axis=0)


def shared_group(half, master, b_pair, b_lo, ones_ref):
    direction = times_left(b_pair, b_lo, half)
    square = direction * direction
    sums = [
        jnp.broadcast_to(jnp.sum(square[p * BLOCK : (p + 1) * BLOCK], axis=0, keepdims=True), (8, GROUP))
        for p in range(2)
    ]
    hi, lo = split(jnp.concatenate(sums, axis=0))
    means = (dot(hi, ones_ref[...]) + dot(lo, ones_ref[...])) * (1.0 / (BLOCK * BLOCK))
    scale = 0.1 * jnp.sqrt(means + 1e-06)
    scale = jnp.concatenate(
        [jnp.broadcast_to(scale[8 * p : 8 * p + 1], (BLOCK, GROUP)) for p in range(2)], axis=0
    )
    update = direction / (jnp.abs(direction) + scale)
    return update, (master - learn_rate * update).astype(bf16)


def sent_place(g):
    from_8, from_19 = (g + 24) // 32, (g + 5) // 24
    return g + 8 * from_8 + from_19 * (26 - 2 * g)


def rep_parts(r):
    return r // 16, (r // 2) % 8, r % 2


def rep_of(x, z, core):
    return x * 16 + z * 2 + core


UNITS = 7
WIDE = 2 * GROUP
Y_AFTER, ONWARD_AFTER, SWAP_AFTER = 2, 4, 6
STEPS = 9
EARLY, MIDDLE = 2, 6


def kernel(
    grads_ref, mom_ref, index_ref, master_ref, table_ref,
    acc, updates, slots,
    grads, kept_rows, wide, own_index, index_rows, places, rows, masters, table,
    in_sem, index_sem, gz_send, gz_recv, gx_send, gx_recv, gs_send, gs_recv,
    m_sem, y_send, y_recv, x_send, x_recv, z_send, z_recv, s_send, s_recv,
):
    rep = lax.axis_index("rep")
    shard = lax.axis_index("fsdp")
    x, z, core = rep_parts(rep)
    cols = masters.shape[1]
    groups = cols // GROUP
    sibling = rep_of(x, z, 1 - core)
    y_peers = [lax.rem(shard + d, 4) for d in range(1, 4)]
    x_peers = [rep_of(lax.rem(x + d, 4), z, core) for d in range(1, 4)]
    z_peers = [rep_of(x, lax.rem(z + d, 8), core) for d in range(1, 8)]
    chunk = PER_STEP * GROUP
    tall = PER_STEP * 2 * BLOCK

    def remote(src, dst, send, recv, peer):
        return pltpu.make_async_remote_copy(
            src_ref=src, dst_ref=dst, send_sem=send, recv_sem=recv, device_id=peer, device_id_type=MESH,
        )


    def columns(step):
        return pl.ds(pl.multiple_of(step * chunk, chunk), chunk)

    def in_copies(step):
        at = columns(step)
        return (
            pltpu.make_async_copy(grads_ref.at[0, :, at], grads.at[:, at], in_sem.at[step, 0]),
            pltpu.make_async_copy(mom_ref.at[0, :, at], acc.at[:, at], in_sem.at[step, 1]),
        )

    def first_group(of_core, unit):
        return 2 * unit + of_core * (groups - 2 - 4 * unit)

    def span(of_core, unit):
        return pl.ds(pl.multiple_of(first_group(of_core, unit) * GROUP, GROUP), WIDE)

    def last_span(of_core):
        return pl.ds(pl.multiple_of((groups // 2 - 1 + 2 * of_core) * GROUP, GROUP), GROUP)

    def master_copy(unit):
        at = span(core, unit)
        return pltpu.make_async_copy(master_ref.at[:, at], masters.at[:, at], m_sem.at[unit])

    pull_own = pltpu.make_async_copy(index_ref.at[x, z, core], own_index, index_sem.at[2])
    pull_table = pltpu.make_async_copy(table_ref, table, index_sem.at[3])
    pulls = [pltpu.make_async_copy(index_ref.at[:, :, c], index_rows.at[c], index_sem.at[c]) for c in range(2)]
    pull_own.start()
    pull_table.start()

    @pl.loop(0, STEPS)
    def _(step):
        for copy in in_copies(step):
            copy.start()

    for pull in pulls:
        pull.start()

    @pl.loop(0, UNITS)
    def _(unit):
        master_copy(unit).start()

    barrier = pltpu.get_barrier_semaphore()
    for peer in y_peers:
        pl.semaphore_signal(barrier, inc=1, device_id={"fsdp": peer}, device_id_type=MESH)
    for peer in x_peers + z_peers + [sibling]:
        pl.semaphore_signal(barrier, inc=1, device_id={"rep": peer}, device_id_type=MESH)


    r_hi, r_lo, rt_hi, rt_lo, ones = (table.at[k * 256 : (k + 1) * 256] for k in range(5))
    l_pair, lt_pair, b_pair = (table.at[1280 + k * 128 : 1408 + k * 128] for k in range(3))
    l_lo, lt_lo = (table.at[1664:1792, k * 128 : (k + 1) * 128] for k in range(2))
    b_lo = table.at[1792:1920, 0:128]
    spread_ref = table.at[1920:1984]

    pull_own.wait()
    row = lax.broadcasted_iota(jnp.int32, (BLOCK, groups * BLOCK), 0)
    lane = lax.broadcasted_iota(jnp.int32, (BLOCK, groups * BLOCK), 1)
    own_slot = (lane & (BAND - 1)) == (row >> 2)
    for p in range(2):
        within = own_index[p : p + 1, :] & 255
        placed = jnp.where(own_slot, jnp.broadcast_to(within, own_slot.shape), 0).astype(f32)
        for g in range(groups):
            at = (2 * g + p) * BLOCK
            wide[at : at + BLOCK, :] = placed[:, g * BLOCK : (g + 1) * BLOCK].astype(bf16)
    pull_table.wait()

    mine = core * 32 + x * 8 + z

    @pl.loop(0, STEPS)
    def _(step):
        for copy in in_copies(step):
            copy.wait()
        at = columns(step)
        total = momentum_decay * acc[:, at] + grads[:, at].astype(f32)
        acc[:, at] = total
        stacked = jnp.concatenate([total[:, g * GROUP : (g + 1) * GROUP] for g in range(PER_STEP)], axis=0)
        half = times_right(stacked, r_hi, r_lo)
        coeff = jnp.concatenate(
            [times_left(l_pair, l_lo, half[g * 128 : (g + 1) * 128]) for g in range(PER_STEP)], axis=0
        )
        tall_at = pl.ds(pl.multiple_of(step * tall, tall), tall)
        index = dot(wide[tall_at, :], spread_ref[...])
        row = lax.broadcasted_iota(jnp.int32, (tall, GROUP), 0)
        lane = lax.broadcasted_iota(jnp.int32, (tall, GROUP), 1)
        place = (((row & 3) << 6) + (lane & 63)).astype(f32)
        kept = jnp.where(index == place, coeff, 0.0)
        kept_rows[tall_at, :] = kept
        hi, mid = split(kept)
        sums = dot_nt(hi, spread_ref[...]) + dot_nt(mid, spread_ref[...])
        zrow = lax.broadcasted_iota(jnp.int32, (tall, BLOCK), 0)
        zlane = lax.broadcasted_iota(jnp.int32, (tall, BLOCK), 1)
        sums = jnp.where((zlane & (BAND - 1)) == ((zrow & 63) >> 2), sums, 0.0)
        for g in range(PER_STEP):
            pair = [
                jnp.sum(sums[(2 * g + p) * BLOCK : (2 * g + p + 1) * BLOCK], axis=0, keepdims=True)
                for p in range(2)
            ]
            rows[mine, pl.ds(sent_place(step * PER_STEP + g), 1), :] = jnp.concatenate(pair, axis=1)

    def inverse_turn(step):
        half = times_right(kept_rows[pl.ds(pl.multiple_of(step * tall, tall), tall), :], rt_hi, rt_lo)
        for g in range(PER_STEP):
            at = pl.ds(pl.multiple_of(step * chunk + g * GROUP, GROUP), GROUP)
            acc[:, at] = acc[:, at] - times_left(lt_pair, lt_lo, half[g * 128 : (g + 1) * 128])


    pl.semaphore_wait(barrier, 14)
    halves_at = (pl.ds(0, 16), pl.ds(16, groups - 16))

    def z_band_copies(h):
        own = rows.at[mine, halves_at[h]]
        return [
            remote(own, own, gz_send.at[h, d], gz_recv.at[h, d], {"rep": peer}) for d, peer in enumerate(z_peers)
        ]

    def bundle(of_x, h):
        return rows.at[pl.ds(core * 32 + of_x * 8, 8), halves_at[h]]

    def x_band_copies(h):
        part = bundle(x, h)
        return [
            remote(part, part, gx_send.at[h, d], gx_recv.at[h, d], {"rep": peer}) for d, peer in enumerate(x_peers)
        ]

    def s_band_copy(h, d):
        part = bundle(lax.rem(x + 4 - d, 4), h)
        return remote(part, part, gs_send.at[h, d], gs_recv.at[h, d], {"rep": sibling})

    def pass_on(h):
        for d, copy in enumerate(x_band_copies(h)):
            copy.wait_recv()
            s_band_copy(h, d + 1).start()

    for h in range(2):
        for copy in z_band_copies(h):
            copy.start()

    for pull in pulls:
        pull.wait()
    for p in range(2):
        for k in range((groups + 1) // 2):
            lanes = min(128, groups * BLOCK - k * 128)
            part = index_rows[:, :, :, p, k * 128 : k * 128 + lanes].reshape(64, lanes)
            turned = part.T & 255
            for b in range(lanes // BAND):
                at = (((2 * k + b // 4) * 2 + p) * 4 + b % 4) * 8
                places[at : at + 8, :] = jnp.concatenate(
                    [turned[b * 16 : b * 16 + 8], turned[b * 16 + 8 : b * 16 + 16]], axis=1
                )
    pl.loop(0, EARLY)(inverse_turn)

    for h in range(2):
        for copy in z_band_copies(h):
            copy.wait()
        for copy in x_band_copies(h):
            copy.start()
        s_band_copy(h, 0).start()
    pl.loop(EARLY, MIDDLE)(inverse_turn)
    pass_on(0)
    for d in range(4):
        s_band_copy(0, d).wait()


    def y_copies(unit):
        at = span(core, unit)
        parts = (
            (pl.ds(0, 32), at),
            (x_rows(x), at),
            z_part(z, unit),
        )
        return [
            remote(
                slots.at[0, rows_at, cols_at], slots.at[d + 1, rows_at, cols_at],
                y_send.at[unit, d, k], y_recv.at[unit, d, k], {"fsdp": y_peers[d]},
            )
            for d in range(3)
            for k, (rows_at, cols_at) in enumerate(parts)
        ]

    def x_rows(of_x):
        return pl.ds(pl.multiple_of(32 + of_x * 16, 16), 16)

    def z_part(of_z, unit):
        start = first_group(core, unit) * GROUP + (of_z % 4) * 128
        return pl.ds(pl.multiple_of(96 + (of_z // 4) * 16, 16), 16), pl.ds(pl.multiple_of(start, 128), 128)

    def onward_copies(unit, arriving):
        at = span(core, unit)
        out = []
        for d in range(3):
            part = slots.at[pl.ds(1, 3), x_rows(lax.rem(x + 3 - d, 4) if arriving else x), at]
            out.append(remote(part, part, x_send.at[unit, d], x_recv.at[unit, d], {"rep": x_peers[d]}))
        for d in range(7):
            rows_at, cols_at = z_part(lax.rem(z + 7 - d, 8) if arriving else z, unit)
            part = slots.at[pl.ds(1, 3), rows_at, cols_at]
            out.append(remote(part, part, z_send.at[unit, d], z_recv.at[unit, d], {"rep": z_peers[d]}))
        return out

    def s_copies(unit, at):
        return [
            remote(part, part, s_send.at[unit, k], s_recv.at[unit, k], {"rep": sibling})
            for k, part in enumerate((slots.at[:, :, at], updates.at[:, at]))
        ]

    def by_width(of_core, unit, act):
        @pl.when(unit < UNITS - 1)
        def _():
            act(span(of_core, unit))

        @pl.when(unit == UNITS - 1)
        def _():
            act(last_span(of_core))

    @pl.loop(0, UNITS + SWAP_AFTER)
    def _(step):
        @pl.when(step == 1)
        def _():
            pass_on(1)

        @pl.when(step == 4)
        def _():
            for d in range(4):
                s_band_copy(1, d).wait()

        @pl.when(step < UNITS)
        def _():
            master_copy(step).wait()
            later = step // 4
            totals = []
            for k in range(2):
                g = first_group(core, step) + k
                early_place = 2 * step + k + core * (9 - 2 * k)
                turned = rows[:, (1 - later) * early_place + later * (g + 8), :].T
                band = jnp.concatenate(
                    [
                        jnp.concatenate([turned[b * 16 : b * 16 + 8], turned[b * 16 + 8 : b * 16 + 16]], axis=1)
                        for b in range(8)
                    ],
                    axis=0,
                )
                lanes = pl.ds(pl.multiple_of(g * 64, 64), 64)
                totals.append(summed_coefficients(band, places[lanes, :]))
            halves_of = times_right(jnp.concatenate(totals, axis=0), rt_hi, rt_lo)
            for k in range(2):
                at = pl.ds(pl.multiple_of((first_group(core, step) + k) * GROUP, GROUP), GROUP)
                update, weights = shared_group(
                    halves_of[k * 2 * BLOCK : (k + 1) * 2 * BLOCK], masters[:, at], b_pair, b_lo, ones
                )
                updates[:, at] = update
                slots[0, :, at] = weights
            for copy in y_copies(step):
                copy.start()

        @pl.when((step >= Y_AFTER) & (step < UNITS + Y_AFTER))
        def _():
            for copy in y_copies(step - Y_AFTER):
                copy.wait_recv()
            for copy in onward_copies(step - Y_AFTER, False):
                copy.start()

        @pl.when((step >= UNITS) & (step < UNITS + STEPS - MIDDLE))
        def _():
            inverse_turn(MIDDLE + step - UNITS)

        @pl.when((step >= ONWARD_AFTER) & (step < UNITS + ONWARD_AFTER))
        def _():
            unit = step - ONWARD_AFTER
            for copy in onward_copies(unit, True):
                copy.wait_recv()

            def act(at):
                for copy in s_copies(unit, at):
                    copy.start()

            by_width(core, unit, act)

        @pl.when(step >= SWAP_AFTER)
        def _():
            unit = step - SWAP_AFTER

            def act(at):
                for copy in s_copies(unit, at):
                    copy.wait_recv()

            by_width(1 - core, unit, act)

    for h in range(2):
        for copy in x_band_copies(h):
            copy.wait_send()

    @pl.loop(0, UNITS)
    def _(unit):
        for copy in y_copies(unit) + onward_copies(unit, False):
            copy.wait_send()

        def drain_own(at):
            for copy in s_copies(unit, at):
                copy.wait_send()

        by_width(core, unit, drain_own)


def table_array():
    t = TABLES
    beside = lambda a, b: np.concatenate([a, b], axis=1)
    parts = [
        *t["right"], *t["right_t"], t["ones"], t["left"][0], t["left_t"][0], t["back"][0],
        beside(t["left"][1], t["left_t"][1]), beside(t["back"][1], t["back"][1]), t["spread"],
    ]
    return jnp.asarray(np.concatenate(parts, axis=0))


def settle(fresh, update, slots):
    rows, cols = update.shape
    part = cols // 9

    def body(fresh_ref, update_ref, slots_ref, fresh_out, update_out, weights_out, sem):
        shard = lax.axis_index("fsdp")
        copies = []
        for n in range(9):
            at = slice(n * part, (n + 1) * part)
            copies.append(pltpu.make_async_copy(fresh_ref.at[:, at], fresh_out.at[0, :, at], sem.at[n, 0]))
            copies.append(pltpu.make_async_copy(update_ref.at[:, at], update_out.at[:, at], sem.at[n, 1]))
        for d in range(4):
            from_shard = lax.rem(shard + 4 - d, 4)
            for n in range(3):
                start = pl.multiple_of(from_shard * cols + n * 3 * part, GROUP)
                copies.append(pltpu.make_async_copy(
                    slots_ref.at[d, :, n * 3 * part : (n + 1) * 3 * part],
                    weights_out.at[:, pl.ds(start, 3 * part)],
                    sem.at[d * 3 + n, 2],
                ))
        for copy in copies:
            copy.start()
        for copy in copies:
            copy.wait()

    anywhere = pl.BlockSpec(memory_space=pl.ANY)
    return tuple(pl.pallas_call(
        body,
        in_specs=[anywhere] * 3,
        out_specs=[anywhere] * 3,
        out_shape=[
            jax.ShapeDtypeStruct((1, rows, cols), f32),
            jax.ShapeDtypeStruct((rows, cols), f32),
            jax.ShapeDtypeStruct((rows, 4 * cols), bf16),
        ],
        scratch_shapes=[pltpu.SemaphoreType.DMA((12, 3))],
        compiler_params=pltpu.CompilerParams(vmem_limit_bytes=2 * 2**20),
    )(fresh, update, slots))


def shards(grads, momentum, master, band_index):
    rows, cols = master.shape
    reps, _, lanes = band_index.shape
    groups = cols // GROUP
    dma = pltpu.SemaphoreType.DMA
    table = table_array()
    anywhere = pl.BlockSpec(memory_space=pl.ANY)
    vmem = pltpu.VMEM
    return settle(*pl.pallas_call(
        kernel,
        in_specs=[anywhere] * 5,
        out_specs=[pl.BlockSpec(memory_space=vmem)] * 3,
        out_shape=[vmem((rows, cols), f32), vmem((rows, cols), f32), vmem((4, rows, cols), bf16)],
        scratch_shapes=[
            vmem((rows, cols), bf16),
            vmem((groups * rows, GROUP), f32),
            vmem((groups * rows, BLOCK), bf16),
            vmem((2, lanes), jnp.int32),
            vmem((2, 4, 8, 2, lanes), jnp.int32),
            vmem((groups * 64, 128), jnp.int32),
            vmem((reps, groups, 128), f32),
            vmem((rows, cols), f32),
            vmem(table.shape, bf16),
            dma((STEPS, 2)), dma((4,)),
            dma((2, 7)), dma((2, 7)), dma((2, 3)), dma((2, 3)), dma((2, 4)), dma((2, 4)),
            dma((UNITS,)), dma((UNITS, 3, 3)), dma((UNITS, 3, 3)), dma((UNITS, 3)), dma((UNITS, 3)),
            dma((UNITS, 7)), dma((UNITS, 7)), dma((UNITS, 2)), dma((UNITS, 2)),
        ],
        compiler_params=pltpu.CompilerParams(
            collective_id=0, has_side_effects=True, vmem_limit_bytes=VMEM_LIMIT
        ),
    )(grads, momentum, band_index.reshape(4, 8, 2, 2, lanes), master, table))


def solution(mesh):
    in_specs = (
        P("rep", None, "fsdp"),
        P("rep", None, "fsdp"),
        P(None, "fsdp"),
        P(None, None, "fsdp"),
    )
    out_specs = (P("rep", None, "fsdp"), P(None, "fsdp"), P())
    return jax.shard_map(shards, mesh=mesh, in_specs=in_specs, out_specs=out_specs, check_vma=False)
```
